32 devices in a mesh: tile: 8 (over y, x, core), src: 4 (over z).
Axes of the slice: x: 2, y: 2, z: 4, core: 2. Of those that a mesh axis runs over, the one named last changes fastest.
Arguments:
- mask_tiles: int32 [128, 512], P('tile'), may hold values 0 or 1
- kernels: bfloat16 [16, 3, 8, 2, 17, 17], P('src'), may hold values from -0.5 to 0.5
- source_weight: int32 [16], P('src'), may hold values from 1 to 8
- dill_rate: float32 [8], P('src'), may hold values from 0.3 to 3
- quencher_load: float32 [8], P('src'), may hold values from 0.1 to 0.5
Outputs:
- acid_field: float32 [8, 128, 512], P('src', 'tile')
- inhibitor: float32 [8, 128, 512], P('src', 'tile')
The draws below stay inside these ranges and needn't reach their ends.
All inputs are finite; a program needn't handle non-finite values. No bound on the sum of `mask_tiles` on one device may be relied on, other than what follows from the above.
Results may differ from the reference program's by a relative error of at most 0.0008.
Values may be sent and summed in bfloat16 or wider, within the bound.
A program may use at most 64 MiB of HBM per device.

```python
import math
import jax
import jax.numpy as jnp
from jax import lax

COLS = 512
KS = 17
DEPTH = 8
STEPS = 8
SOURCES = 16
NROWS = 128


def set_ends(drawn, stream_key, low, high):
    place = [jax.random.randint(jax.random.fold_in(stream_key, axis), (), 0, length) for axis, length in enumerate(drawn.shape)]
    main_axis = drawn.shape.index(max(drawn.shape))
    next_to = place[:main_axis] + [(place[main_axis] + 1) % drawn.shape[main_axis]] + place[main_axis + 1:]
    return drawn.at[tuple(place)].set(low).at[tuple(next_to)].set(high)


def block_levels(stream_key, dims, pieces, low, largest):
    factor_of = 1.0
    for axis_at, parts in pieces:
        heights = jax.random.uniform(jax.random.fold_in(jax.random.fold_in(stream_key, 6), axis_at), (parts,), jnp.float32, low / len(pieces), largest / len(pieces))
        factor_of = factor_of * jnp.repeat(jnp.exp(heights), dims[axis_at] // parts).reshape((-1,) + (1,) * (len(dims) - 1 - axis_at))
    return factor_of


def gaussian(stream_key, extent, deviation, bound, pieces=(), held_as=jnp.bfloat16):
    result = deviation * jax.random.normal(stream_key, extent, jnp.float32)
    if pieces:
        result = result * block_levels(stream_key, extent, pieces, -0.22, 0.18)
    return jnp.clip(result, -bound, bound).astype(held_as)


def setup_inputs(seed: int = 0) -> dict:
    streams_of = jax.random.split(jax.random.key(seed), 6)
    return {
        "mask_tiles": set_ends((jax.random.randint(streams_of[0], (NROWS, COLS), 0, 2) < 1).astype(jnp.int32), jax.random.fold_in(streams_of[0], 1), 0, 1),
        "kernels": gaussian(streams_of[1], (SOURCES, 3, DEPTH, 2, KS, KS), (KS * KS // 2) ** -0.5, 0.5, ((0, 4),)),
        "source_weight": set_ends(jax.random.randint(streams_of[2], (SOURCES,), 1, 9), jax.random.fold_in(streams_of[2], 1), 1, 8).astype(jnp.int32),
        "dill_rate": jnp.clip(jnp.exp(math.log(3.0) - 2.3025851 * jax.random.uniform(streams_of[3], (DEPTH,), jnp.float32) ** block_levels(streams_of[3], (DEPTH,), ((0, 4),), -0.2, 0.2)), 0.3, 3.0),
        "quencher_load": jnp.clip(0.1 + 0.4 * jax.random.uniform(streams_of[4], (DEPTH,), jnp.float32) ** block_levels(streams_of[4], (DEPTH,), ((0, 4),), -0.2, 0.2), 0.1, 0.5),
    }


acid_lateral = 0.15
acid_vertical = 0.12
quench_lateral = 0.05
quench_vertical = 0.04
react_rate = 0.3
deprotect_rate = 0.25


def advance(extended):
    centre = extended[:, 1:-1, 1:-1]
    padded_cols = jnp.pad(centre, ((0, 0), (0, 0), (0, 0), (1, 1)))
    lateral = extended[:, 1:-1, 2:] + extended[:, 1:-1, :-2] + padded_cols[..., 2:] + padded_cols[..., :-2] - 4.0 * centre
    vertical = extended[:, 2:, 1:-1] + extended[:, :-2, 1:-1] - 2.0 * centre
    acid_now = centre[0]
    quench_now = centre[1]
    reacted = react_rate * acid_now * quench_now
    acid_next = acid_now + acid_lateral * lateral[0] + acid_vertical * vertical[0] - reacted
    quench_next = quench_now + quench_lateral * lateral[1] + quench_vertical * vertical[1] - reacted
    return jnp.stack([acid_next, quench_next])


def reference(mask_tiles, kernels, source_weight, dill_rate, quencher_load):
    rim_width = KS // 2
    binary = mask_tiles.astype(jnp.bfloat16)
    padded = jnp.pad(binary, ((rim_width, rim_width), (rim_width, rim_width)))
    frame_band = padded[None, None]

    def one_source(running, source_item):
        kernel_block, weight_value = source_item
        filters = kernel_block.reshape(3 * DEPTH * 2, 1, KS, KS)
        fields = lax.conv_general_dilated(frame_band, filters, (1, 1), "VALID", preferred_element_type=jnp.float32)[0]
        squares = (fields * fields).reshape(3, DEPTH, 2, NROWS, COLS).sum(axis=(0, 2))
        return running + weight_value.astype(jnp.float32) * squares, None

    start_value = jnp.zeros((DEPTH, NROWS, COLS), jnp.float32)
    summed = lax.scan(one_source, start_value, (kernels, source_weight))[0]
    intensity = summed * (1.0 / (24.0 * SOURCES))
    acid_start = 1.0 - jnp.exp(-dill_rate[:, None, None] * intensity)
    quench_start = jnp.broadcast_to(quencher_load[:, None, None], acid_start.shape)
    bake_state = jnp.stack([acid_start, quench_start])
    dose_sum = jnp.zeros_like(acid_start)
    for substep in range(STEPS):
        row_padded = jnp.pad(bake_state, ((0, 0), (0, 0), (1, 1), (0, 0)))
        extended = jnp.concatenate([row_padded[:, :1], row_padded, row_padded[:, -1:]], axis=1)
        bake_state = advance(extended)
        dose_sum = dose_sum + bake_state[0]
    inhibitor = jnp.exp(-deprotect_rate * dose_sum)
    return bake_state[0], inhibitor
```

```python
import functools

import jax
import jax.numpy as jnp
from jax import lax
from jax.experimental import pallas as pl
from jax.experimental.pallas import tpu as pltpu
from jax.sharding import PartitionSpec as P

STEPS = 8
SLAB = 24
DEEP = 512
MARGIN = 64

acid_lateral = 0.15
acid_vertical = 0.12
quench_lateral = 0.05
quench_vertical = 0.04
react_rate = 0.3
deprotect_rate = 0.25

MESH = pl.DeviceIdType.MESH


def kernel(
    dims,
    mask_ref, filt_ref, load_ref, dill_ref, acid_ref, inhib_ref,
    above, below, filters, loads, shifted, light, light_out, light_in,
    acid, quench, dose, final_out, final_in,
    mask_send, mask_recv, filt_send, filt_recv, load_send, load_recv,
    light_send, light_recv, final_send, final_recv,
):
    tiles, srcs, rows, cols, side, planes, scale = dims
    rim = side // 2
    halo = STEPS
    tall = rows + 2 * halo
    block = cols // srcs
    wide = block + 2 * MARGIN
    tile = lax.axis_index("tile")
    src = lax.axis_index("src")
    has_above = tile > 0
    has_below = tile < tiles - 1

    barrier = pltpu.get_barrier_semaphore()
    peers = [lax.rem(src + step, srcs) for step in range(1, srcs)]
    for peer in peers:
        pl.semaphore_signal(barrier, inc=1, device_id=(tile, peer), device_id_type=MESH)

    @pl.when(has_above)
    def _():
        pl.semaphore_signal(barrier, inc=1, device_id=(tile - 1, src), device_id_type=MESH)

    @pl.when(has_below)
    def _():
        pl.semaphore_signal(barrier, inc=1, device_id=(tile + 1, src), device_id_type=MESH)

    greeted = srcs - 1 + jnp.where(has_above, 1, 0) + jnp.where(has_below, 1, 0)
    pl.semaphore_wait(barrier, greeted)

    def to_above():
        return pltpu.make_async_remote_copy(
            mask_ref, below, mask_send.at[0], mask_recv.at[0],
            device_id=(tile - 1, src), device_id_type=MESH)

    def to_below():
        return pltpu.make_async_remote_copy(
            mask_ref, above, mask_send.at[1], mask_recv.at[1],
            device_id=(tile + 1, src), device_id_type=MESH)

    @pl.when(has_above)
    def _():
        to_above().start()

    @pl.when(has_below)
    def _():
        to_below().start()

    filt_copies = []
    load_copies = []
    for at, peer in enumerate(peers):
        copy = pltpu.make_async_remote_copy(
            filt_ref.at[peer], filters.at[src], filt_send.at[at], filt_recv.at[at],
            device_id=(tile, peer), device_id_type=MESH)
        copy.start()
        filt_copies.append(copy)
        copy = pltpu.make_async_remote_copy(
            load_ref, loads.at[src], load_send.at[at], load_recv.at[at],
            device_id=(tile, peer), device_id_type=MESH)
        copy.start()
        load_copies.append(copy)
    filters[src] = filt_ref[src]
    loads[src] = load_ref[...]
    shifted[...] = jnp.zeros_like(shifted)

    @pl.when(jnp.logical_not(has_above))
    def _():
        above[...] = jnp.zeros_like(above)

    @pl.when(jnp.logical_not(has_below))
    def _():
        below[...] = jnp.zeros_like(below)

    @pl.when(has_above)
    def _():
        to_above().wait_send()
        to_below().wait_recv()

    @pl.when(has_below)
    def _():
        to_below().wait_send()
        to_above().wait_recv()

    image = jnp.concatenate([above[...], mask_ref[...], below[...]], axis=0).astype(jnp.float32)
    ring = jnp.concatenate([image, jnp.zeros((image.shape[0], 128), jnp.float32)], axis=1)
    length = cols + 128
    for b in range(side):
        moved = pltpu.roll(ring, (rim - b) % length, 1)[:, :cols]
        for c in range(cols // 128):
            shifted[c, pl.ds(b, image.shape[0], SLAB), :] = moved[:, c * 128:(c + 1) * 128]

    for copy in filt_copies + load_copies:
        copy.wait()

    held = filters[...].reshape(-1, DEEP).astype(jnp.float32)
    lane = lax.broadcasted_iota(jnp.int32, held.shape, 1)
    weights = jnp.sum(jnp.where(lane == DEEP - 1, held, 0.0), axis=1, keepdims=True)
    taps = jnp.where(lane < side * SLAB, held, 0.0).astype(jnp.bfloat16)
    group = held.shape[0] // (srcs * planes)
    first = rows - halo - rim

    def one_row(r, carry):
        start = pl.multiple_of((r + first) * SLAB, 8)
        patch = jnp.concatenate(
            [shifted[c, pl.ds(start, DEEP), :] for c in range(cols // 128)], axis=1
        ).astype(jnp.bfloat16)
        field = jnp.dot(taps, patch, preferred_element_type=jnp.float32)
        power = (field * field * weights).reshape(srcs, planes, group, cols)
        for k in range(planes):
            light[k, pl.ds(r, 1), :] = jnp.sum(
                power[:, k].reshape(srcs * group, cols), axis=0, keepdims=True)
        return carry

    lax.fori_loop(0, tall, one_row, 0)

    for k in range(planes):
        exposed = light[k] * (dill_ref[k] * scale)
        exposed = jnp.concatenate([exposed, jnp.zeros((tall, 2 * MARGIN), jnp.float32)], axis=1)
        exposed = pltpu.roll(exposed, MARGIN, 1)
        for s in range(srcs):
            light_out[s, k] = exposed[:, s * block:s * block + wide].astype(jnp.bfloat16)
    light_in[src] = light_out[src]
    copies = []
    for at, peer in enumerate(peers):
        copy = pltpu.make_async_remote_copy(
            light_out.at[peer], light_in.at[src], light_send.at[at], light_recv.at[at],
            device_id=(tile, peer), device_id_type=MESH)
        copy.start()
        copies.append(copy)
    row = lax.broadcasted_iota(jnp.int32, (tall, wide), 0) + (tile * rows - halo)
    col = lax.broadcasted_iota(jnp.int32, (tall, wide), 1) + (src * block - MARGIN)
    inside = (row >= 0) & (row < tiles * rows) & (col >= 0) & (col < cols)
    inside = jnp.where(inside, 1.0, 0.0)
    for copy in copies:
        copy.wait()

    depth = srcs * planes
    for k in range(depth):
        exposed = light_in[k // planes, k % planes].astype(jnp.float32)
        acid[0, k] = (1.0 - jnp.exp(-exposed)) * inside
        quench[0, k] = loads[k // planes, k % planes:k % planes + 1, 0:1] * inside
        dose[k] = jnp.zeros((tall, wide), jnp.float32)

    def spread(held, now, k, lateral_rate, vertical_rate):
        centre = held[now, k]
        sides = (
            pltpu.roll(centre, 1, 0) + pltpu.roll(centre, tall - 1, 0)
            + pltpu.roll(centre, 1, 1) + pltpu.roll(centre, wide - 1, 1)
        )
        lateral = sides - 4.0 * centre
        vertical = held[now, min(k + 1, depth - 1)] + held[now, max(k - 1, 0)] - 2.0 * centre
        return centre, centre + lateral_rate * lateral + vertical_rate * vertical

    def two_steps(pair, carry):
        for now in range(2):
            for k in range(depth):
                a, a_next = spread(acid, now, k, acid_lateral, acid_vertical)
                q, q_next = spread(quench, now, k, quench_lateral, quench_vertical)
                reacted = react_rate * a * q
                a_next = (a_next - reacted) * inside
                acid[1 - now, k] = a_next
                quench[1 - now, k] = (q_next - reacted) * inside
                dose[k] = dose[k] + a_next
        return carry

    lax.fori_loop(0, STEPS // 2, two_steps, 0)

    for k in range(depth):
        for which, whole in enumerate((acid[0, k], jnp.exp(-deprotect_rate * dose[k]))):
            final_out[k // planes, which, k % planes] = pltpu.roll(
                whole, wide - MARGIN, 1)[halo:halo + rows, :block]
    copies = []
    for at, peer in enumerate(peers):
        copy = pltpu.make_async_remote_copy(
            final_out.at[peer], final_in.at[src], final_send.at[at], final_recv.at[at],
            device_id=(tile, peer), device_id_type=MESH)
        copy.start()
        copies.append(copy)
    final_in[src] = final_out[src]
    for copy in copies:
        copy.wait()
    for s in range(srcs):
        acid_ref[:, :, s * block:(s + 1) * block] = final_in[s, 0]
        inhib_ref[:, :, s * block:(s + 1) * block] = final_in[s, 1]


def shards(mask_tiles, kernels, source_weight, dill_rate, quencher_load):
    tiles, srcs = lax.axis_size("tile"), lax.axis_size("src")
    rows, cols = mask_tiles.shape
    planes = dill_rate.shape[0]
    points, parts, depth, quad, side, _ = kernels.shape
    group = points * parts * quad
    taps = jnp.pad(kernels, ((0, 0),) * 5 + ((0, SLAB - side),))
    taps = taps.reshape(points, parts, srcs, planes, quad, side * SLAB)
    spare = DEEP - side * SLAB
    last = jnp.arange(spare) == spare - 1
    tail = jnp.where(last, source_weight.astype(jnp.bfloat16)[:, None, None, None, None, None], 0)
    tail = jnp.broadcast_to(tail.astype(jnp.bfloat16), taps.shape[:-1] + (spare,))
    taps = jnp.concatenate([taps, tail], axis=-1)
    taps = taps.transpose(2, 3, 0, 1, 4, 5).reshape(srcs, planes * group, DEEP)
    loads = jnp.broadcast_to(jnp.pad(quencher_load, (0, 8 - planes))[:, None], (8, 128))
    dims = (tiles, srcs, rows, cols, side, planes, 1.0 / (24.0 * points * srcs))
    tall = rows + 2 * STEPS
    block = cols // srcs
    wide = block + 2 * MARGIN
    depth_all = srcs * planes
    f32 = jnp.float32
    image_rows = 3 * rows
    first = rows - STEPS - side // 2
    deep_rows = max(image_rows * SLAB, (first + tall - 1) * SLAB + DEEP)
    out = jax.ShapeDtypeStruct((planes, rows, cols), f32)
    vmem = pl.BlockSpec(memory_space=pltpu.VMEM)
    dma = pltpu.SemaphoreType.DMA
    return pl.pallas_call(
        functools.partial(kernel, dims),
        out_shape=(out, out),
        in_specs=[vmem, vmem, vmem, pl.BlockSpec(memory_space=pltpu.SMEM)],
        out_specs=(vmem, vmem),
        scratch_shapes=[
            pltpu.VMEM((rows, cols), jnp.int32),
            pltpu.VMEM((rows, cols), jnp.int32),
            pltpu.VMEM((srcs, planes * group, DEEP), jnp.bfloat16),
            pltpu.VMEM((srcs, 8, 128), f32),
            pltpu.VMEM((cols // 128, deep_rows, 128), f32),
            pltpu.VMEM((planes, tall, cols), f32),
            pltpu.VMEM((srcs, planes, tall, wide), jnp.bfloat16),
            pltpu.VMEM((srcs, planes, tall, wide), jnp.bfloat16),
            pltpu.VMEM((2, depth_all, tall, wide), f32),
            pltpu.VMEM((2, depth_all, tall, wide), f32),
            pltpu.VMEM((depth_all, tall, wide), f32),
            pltpu.VMEM((srcs, 2, planes, rows, block), f32),
            pltpu.VMEM((srcs, 2, planes, rows, block), f32),
            dma((2,)), dma((2,)),
            dma((srcs - 1,)), dma((srcs - 1,)),
            dma((srcs - 1,)), dma((srcs - 1,)),
            dma((srcs - 1,)), dma((srcs - 1,)),
            dma((srcs - 1,)), dma((srcs - 1,)),
        ],
        compiler_params=pltpu.CompilerParams(
            collective_id=0, has_side_effects=True, vmem_limit_bytes=40 * 1024 * 1024
        ),
    )(mask_tiles, taps, loads, dill_rate)


def solution(mesh):
    in_specs = (
        P("tile", None),
        P("src", None, None, None, None, None),
        P("src"),
        P("src"),
        P("src"),
    )
    out_specs = (P("src", "tile", None), P("src", "tile", None))
    return jax.shard_map(shards, mesh=mesh, in_specs=in_specs, out_specs=out_specs, check_vma=False)
```

```python
import functools

import jax
import jax.numpy as jnp
from jax import lax
from jax.experimental import pallas as pl
from jax.experimental.pallas import tpu as pltpu
from jax.sharding import PartitionSpec as P

STEPS = 8
SLAB = 21
DEEP = 512
WIRE = 384
GROUP = 8
MARGIN = 64

acid_lateral = 0.15
acid_vertical = 0.12
quench_lateral = 0.05
quench_vertical = 0.04
react_rate = 0.3
deprotect_rate = 0.25

MESH = pl.DeviceIdType.MESH


def kernel(
    dims,
    mask_ref, raw_ref, pupil_ref, dill_ref, quench_ref, acid_ref, inhib_ref,
    above, below, unsorted, sorted_rows, filt_out, load_out, filters, loads, shifted, patches, taps,
    light, light_out, light_in,
    acid, quench, dose, final_out, final_in,
    mask_send, mask_recv, filt_send, filt_recv, load_send, load_recv,
    light_send, light_recv, final_send, final_recv,
):
    tiles, srcs, rows, cols, side, planes, scale = dims
    rim = side // 2
    halo = STEPS
    tall = rows + 2 * halo
    block = cols // srcs
    wide = block + 2 * MARGIN
    tile = lax.axis_index("tile")
    src = lax.axis_index("src")
    has_above = tile > 0
    has_below = tile < tiles - 1

    barrier = pltpu.get_barrier_semaphore()
    peers = [lax.rem(src + step, srcs) for step in range(1, srcs)]
    for peer in peers:
        pl.semaphore_signal(barrier, inc=1, device_id=(tile, peer), device_id_type=MESH)

    @pl.when(has_above)
    def _():
        pl.semaphore_signal(barrier, inc=1, device_id=(tile - 1, src), device_id_type=MESH)

    @pl.when(has_below)
    def _():
        pl.semaphore_signal(barrier, inc=1, device_id=(tile + 1, src), device_id_type=MESH)

    lanes = 128
    points, parts = pupil_ref.shape[0], raw_ref.shape[0] // (2 * side * srcs * planes * pupil_ref.shape[0])
    channels = srcs * planes * points * parts
    share = planes * points * parts
    lane = lax.broadcasted_iota(jnp.int32, (channels, lanes), 1)
    point = lax.broadcasted_iota(jnp.int32, (channels, lanes), 0) // (srcs * planes * parts)
    weight = jnp.zeros((channels, lanes), jnp.float32)
    for p in range(points):
        weight = jnp.where(point == p, pupil_ref[p].astype(jnp.float32), weight)
    weight = jnp.where(lane == lanes - 1, weight, 0.0)
    for q in range(2):
        strips = [jnp.zeros((channels, lanes), jnp.float32) for _ in range(WIRE // lanes)]
        strips[-1] = weight
        for a in range(side):
            part = raw_ref[pl.ds(2 * a + q, channels, 2 * side), :]
            at, offset = divmod(a * SLAB, lanes)
            if offset:
                part = pltpu.roll(part, offset, 1)
            if offset + side > lanes:
                strips[at + 1] = strips[at + 1] + jnp.where(lane < offset, part, 0.0)
                part = jnp.where(lane >= offset, part, 0.0)
            strips[at] = strips[at] + part
        for c, strip in enumerate(strips):
            unsorted[q, c] = strip
            for k in range(srcs * planes):
                sorted_rows[q, c, k * points * parts:(k + 1) * points * parts] = unsorted[
                    q, c, pl.ds(k, points * parts, srcs * planes), :]
            for s in range(srcs):
                filt_out[s, q * share:(q + 1) * share, c * lanes:(c + 1) * lanes] = sorted_rows[
                    q, c, s * share:(s + 1) * share].astype(jnp.bfloat16)
    plane = lax.broadcasted_iota(jnp.int32, load_out.shape, 0)
    spread_load = jnp.zeros(load_out.shape, jnp.float32)
    for k in range(planes):
        spread_load = jnp.where(plane == k, quench_ref[k], spread_load)
    load_out[...] = spread_load

    greeted = srcs - 1 + jnp.where(has_above, 1, 0) + jnp.where(has_below, 1, 0)
    pl.semaphore_wait(barrier, greeted)

    def to_above():
        return pltpu.make_async_remote_copy(
            mask_ref, below, mask_send.at[0], mask_recv.at[0],
            device_id=(tile - 1, src), device_id_type=MESH)

    def to_below():
        return pltpu.make_async_remote_copy(
            mask_ref, above, mask_send.at[1], mask_recv.at[1],
            device_id=(tile + 1, src), device_id_type=MESH)

    @pl.when(has_above)
    def _():
        to_above().start()

    @pl.when(has_below)
    def _():
        to_below().start()

    filt_copies = []
    load_copies = []
    for at, peer in enumerate(peers):
        copy = pltpu.make_async_remote_copy(
            filt_out.at[peer], filters.at[src], filt_send.at[at], filt_recv.at[at],
            device_id=(tile, peer), device_id_type=MESH)
        copy.start()
        filt_copies.append(copy)
        copy = pltpu.make_async_remote_copy(
            load_out, loads.at[src], load_send.at[at], load_recv.at[at],
            device_id=(tile, peer), device_id_type=MESH)
        copy.start()
        load_copies.append(copy)
    filters[src] = filt_out[src]
    loads[src] = load_out[...]
    shifted[...] = jnp.zeros_like(shifted)

    @pl.when(jnp.logical_not(has_above))
    def _():
        above[...] = jnp.zeros_like(above)

    @pl.when(jnp.logical_not(has_below))
    def _():
        below[...] = jnp.zeros_like(below)

    @pl.when(has_above)
    def _():
        to_above().wait_send()
        to_below().wait_recv()

    @pl.when(has_below)
    def _():
        to_below().wait_send()
        to_above().wait_recv()

    image = jnp.concatenate([above[...], mask_ref[...], below[...]], axis=0).astype(jnp.float32)
    ring = jnp.concatenate([image, jnp.zeros((image.shape[0], 128), jnp.float32)], axis=1)
    length = cols + 128
    for b in range(side):
        moved = pltpu.roll(ring, (rim - b) % length, 1)[:, :cols]
        for c in range(cols // 128):
            shifted[c, pl.ds(b, image.shape[0], SLAB), :] = moved[:, c * 128:(c + 1) * 128]

    for g in range(tall // GROUP):
        for c in range(cols // 128):
            patches[g, :, c * 128:(c + 1) * 128] = shifted[
                c, g * GROUP * SLAB:g * GROUP * SLAB + DEEP, :].astype(jnp.bfloat16)
    light[...] = jnp.zeros_like(light)

    place = lax.broadcasted_iota(jnp.int32, (2 * share, WIRE), 1)
    ours = lax.broadcasted_iota(jnp.int32, (share, cols), 0) // (points * parts)
    for step in range(srcs):
        if step:
            filt_copies[step - 1].wait_recv()
        held = filters[lax.rem(src + srcs - step, srcs)].astype(jnp.float32)
        weights = jnp.sum(jnp.where(place == WIRE - 1, held, 0.0), axis=1, keepdims=True)[:share]
        held = jnp.where(place < side * SLAB, held, 0.0)
        held = jnp.concatenate([held, jnp.zeros((2 * share, DEEP - WIRE), jnp.float32)], axis=1)
        for r in range(GROUP):
            moved = pltpu.roll(held, r * SLAB, 1) if r else held
            taps[r * 2 * share:(r + 1) * 2 * share] = moved.astype(jnp.bfloat16)

        def one_group(g, carry):
            field = jnp.dot(taps[...], patches[g], preferred_element_type=jnp.float32)
            square = (field * field).reshape(GROUP, 2, share, cols)
            power = (square[:, 0] + square[:, 1]) * weights
            start = pl.multiple_of(g * GROUP, GROUP)
            for k in range(planes):
                own = jnp.where(ours == k, power, 0.0)
                light[k, pl.ds(start, GROUP), :] += jnp.sum(own, axis=1)
            return carry

        lax.fori_loop(0, tall // GROUP, one_group, 0)
    for copy in load_copies:
        copy.wait()
    for copy in filt_copies:
        copy.wait_send()

    for k in range(planes):
        exposed = light[k] * (dill_ref[k] * scale)
        exposed = jnp.concatenate([exposed, jnp.zeros((tall, 2 * MARGIN), jnp.float32)], axis=1)
        exposed = pltpu.roll(exposed, MARGIN, 1)
        for s in range(srcs):
            light_out[s, k] = exposed[:, s * block:s * block + wide].astype(jnp.bfloat16)
    light_in[src] = light_out[src]
    copies = []
    for at, peer in enumerate(peers):
        copy = pltpu.make_async_remote_copy(
            light_out.at[peer], light_in.at[src], light_send.at[at], light_recv.at[at],
            device_id=(tile, peer), device_id_type=MESH)
        copy.start()
        copies.append(copy)
    row = lax.broadcasted_iota(jnp.int32, (tall, wide), 0) + (tile * rows - halo)
    col = lax.broadcasted_iota(jnp.int32, (tall, wide), 1) + (src * block - MARGIN)
    inside = (row >= 0) & (row < tiles * rows) & (col >= 0) & (col < cols)
    inside = jnp.where(inside, 1.0, 0.0)
    for copy in copies:
        copy.wait()

    depth = srcs * planes
    for k in range(depth):
        exposed = light_in[k // planes, k % planes].astype(jnp.float32)
        acid[0, k] = (1.0 - jnp.exp(-exposed)) * inside
        quench[0, k] = loads[k // planes, k % planes:k % planes + 1, 0:1] * inside
        dose[k] = jnp.zeros((tall, wide), jnp.float32)

    def spread(held, now, k, lateral_rate, vertical_rate):
        centre = held[now, k]
        sides = (
            pltpu.roll(centre, 1, 0) + pltpu.roll(centre, tall - 1, 0)
            + pltpu.roll(centre, 1, 1) + pltpu.roll(centre, wide - 1, 1)
        )
        vertical = held[now, min(k + 1, depth - 1)] + held[now, max(k - 1, 0)]
        stay = 1.0 - 4.0 * lateral_rate - 2.0 * vertical_rate
        return centre, stay * centre + lateral_rate * sides + vertical_rate * vertical

    def two_steps(pair, carry):
        for now in range(2):
            for k in range(depth):
                a, a_next = spread(acid, now, k, acid_lateral, acid_vertical)
                q, q_next = spread(quench, now, k, quench_lateral, quench_vertical)
                reacted = react_rate * a * q
                a_next = (a_next - reacted) * inside
                acid[1 - now, k] = a_next
                quench[1 - now, k] = (q_next - reacted) * inside
                dose[k] = dose[k] + a_next
        return carry

    lax.fori_loop(0, STEPS // 2, two_steps, 0)

    for k in range(depth):
        for which, whole in enumerate((acid[0, k], jnp.exp(-deprotect_rate * dose[k]))):
            final_out[k // planes, which, k % planes] = pltpu.roll(
                whole, wide - MARGIN, 1)[halo:halo + rows, :block]
    copies = []
    for at, peer in enumerate(peers):
        copy = pltpu.make_async_remote_copy(
            final_out.at[peer], final_in.at[src], final_send.at[at], final_recv.at[at],
            device_id=(tile, peer), device_id_type=MESH)
        copy.start()
        copies.append(copy)
    final_in[src] = final_out[src]
    for copy in copies:
        copy.wait()
    for s in range(srcs):
        acid_ref[:, :, s * block:(s + 1) * block] = final_in[s, 0]
        inhib_ref[:, :, s * block:(s + 1) * block] = final_in[s, 1]


def shards(mask_tiles, kernels, source_weight, dill_rate, quencher_load):
    tiles, srcs = lax.axis_size("tile"), lax.axis_size("src")
    rows, cols = mask_tiles.shape
    planes = dill_rate.shape[0]
    points, parts, depth, quad, side, _ = kernels.shape
    share = planes * points * parts
    raw = kernels.transpose(0, 1, 2, 4, 3, 5).astype(jnp.float32)
    raw = jnp.pad(raw, ((0, 0),) * 5 + ((0, 128 - side),)).reshape(-1, 128)
    dims = (tiles, srcs, rows, cols, side, planes, 1.0 / (24.0 * points * srcs))
    tall = rows + 2 * STEPS
    block = cols // srcs
    wide = block + 2 * MARGIN
    depth_all = srcs * planes
    f32 = jnp.float32
    image_rows = 3 * rows
    deep_rows = max(image_rows * SLAB, (tall - GROUP) * SLAB + DEEP)
    out = jax.ShapeDtypeStruct((planes, rows, cols), f32)
    vmem = pl.BlockSpec(memory_space=pltpu.VMEM)
    smem = pl.BlockSpec(memory_space=pltpu.SMEM)
    dma = pltpu.SemaphoreType.DMA
    return pl.pallas_call(
        functools.partial(kernel, dims),
        out_shape=(out, out),
        in_specs=[vmem, vmem, smem, smem, smem],
        out_specs=(vmem, vmem),
        scratch_shapes=[
            pltpu.VMEM((rows, cols), jnp.int32),
            pltpu.VMEM((rows, cols), jnp.int32),
            pltpu.VMEM((2, WIRE // 128, srcs * share, 128), f32),
            pltpu.VMEM((2, WIRE // 128, srcs * share, 128), f32),
            pltpu.VMEM((srcs, 2 * share, WIRE), jnp.bfloat16),
            pltpu.VMEM((8, 128), f32),
            pltpu.VMEM((srcs, 2 * share, WIRE), jnp.bfloat16),
            pltpu.VMEM((srcs, 8, 128), f32),
            pltpu.VMEM((cols // 128, deep_rows, 128), f32),
            pltpu.VMEM((tall // GROUP, DEEP, cols), jnp.bfloat16),
            pltpu.VMEM((GROUP * 2 * share, DEEP), jnp.bfloat16),
            pltpu.VMEM((planes, tall, cols), f32),
            pltpu.VMEM((srcs, planes, tall, wide), jnp.bfloat16),
            pltpu.VMEM((srcs, planes, tall, wide), jnp.bfloat16),
            pltpu.VMEM((2, depth_all, tall, wide), f32),
            pltpu.VMEM((2, depth_all, tall, wide), f32),
            pltpu.VMEM((depth_all, tall, wide), f32),
            pltpu.VMEM((srcs, 2, planes, rows, block), f32),
            pltpu.VMEM((srcs, 2, planes, rows, block), f32),
            dma((2,)), dma((2,)),
            dma((srcs - 1,)), dma((srcs - 1,)),
            dma((srcs - 1,)), dma((srcs - 1,)),
            dma((srcs - 1,)), dma((srcs - 1,)),
            dma((srcs - 1,)), dma((srcs - 1,)),
        ],
        compiler_params=pltpu.CompilerParams(
            collective_id=0, has_side_effects=True, vmem_limit_bytes=40 * 1024 * 1024
        ),
    )(mask_tiles, raw, source_weight, dill_rate, quencher_load)


def solution(mesh):
    in_specs = (
        P("tile", None),
        P("src", None, None, None, None, None),
        P("src"),
        P("src"),
        P("src"),
    )
    out_specs = (P("src", "tile", None), P("src", "tile", None))
    return jax.shard_map(shards, mesh=mesh, in_specs=in_specs, out_specs=out_specs, check_vma=False)
```

```python
import functools

import jax
import jax.numpy as jnp
from jax import lax
from jax.experimental import pallas as pl
from jax.experimental.pallas import tpu as pltpu
from jax.sharding import PartitionSpec as P

STEPS = 8
SLAB = 21
DEEP = 512
WIRE = 384
GROUP = 8

acid_lateral = 0.15
acid_vertical = 0.12
quench_lateral = 0.05
quench_vertical = 0.04
react_rate = 0.3
deprotect_rate = 0.25

MESH = pl.DeviceIdType.MESH


def kernel(
    dims,
    mask_ref, raw_ref, pupil_ref, dill_ref, quench_ref, acid_ref, inhib_ref,
    above, below, raw, unsorted, sorted_rows, filt_out, load_out, filters, loads, shifted, patches, taps,
    light, light_out, light_in, rim_out, rim_in,
    acid, quench, dose, final_out, final_in,
    mask_send, mask_recv, filt_send, filt_recv, load_send, load_recv,
    light_send, light_recv, rim_send, rim_recv, final_send, final_recv,
):
    tiles, srcs, rows, cols, side, planes, scale = dims
    rim = side // 2
    halo = STEPS
    tall = rows + 2 * halo
    block = cols // srcs
    wide = block + 128
    tile = lax.axis_index("tile")
    src = lax.axis_index("src")
    has_above = tile > 0
    has_below = tile < tiles - 1

    barrier = pltpu.get_barrier_semaphore()
    peers = [lax.rem(src + step, srcs) for step in range(1, srcs)]
    for peer in peers:
        pl.semaphore_signal(barrier, inc=1, device_id=(tile, peer), device_id_type=MESH)

    @pl.when(has_above)
    def _():
        pl.semaphore_signal(barrier, inc=1, device_id=(tile - 1, src), device_id_type=MESH)

    @pl.when(has_below)
    def _():
        pl.semaphore_signal(barrier, inc=1, device_id=(tile + 1, src), device_id_type=MESH)

    lanes = 128
    points, parts = pupil_ref.shape[0], raw_ref.shape[0] // (2 * side * srcs * planes * pupil_ref.shape[0])
    channels = srcs * planes * points * parts
    share = planes * points * parts
    lane = lax.broadcasted_iota(jnp.int32, (channels, lanes), 1)
    point = lax.broadcasted_iota(jnp.int32, (channels, lanes), 0) // (srcs * planes * parts)
    weight = jnp.zeros((channels, lanes), jnp.float32)
    for p in range(points):
        weight = jnp.where(point == p, pupil_ref[p].astype(jnp.float32), weight)
    weight = jnp.where(lane == lanes - 1, weight, 0.0)
    raw[...] = jnp.zeros_like(raw)

    def widen(at, carry):
        here = pl.ds(pl.multiple_of(at * channels, channels), channels)
        raw[here, :side] = raw_ref[here, :].astype(jnp.float32)
        return carry

    lax.fori_loop(0, 2 * side, widen, 0)
    for q in range(2):
        strips = [jnp.zeros((channels, lanes), jnp.float32) for _ in range(WIRE // lanes)]
        strips[-1] = weight
        for a in range(side):
            part = raw[pl.ds(2 * a + q, channels, 2 * side), :]
            at, offset = divmod(a * SLAB, lanes)
            if offset:
                part = pltpu.roll(part, offset, 1)
            if offset + side > lanes:
                strips[at + 1] = strips[at + 1] + jnp.where(lane < offset, part, 0.0)
                part = jnp.where(lane >= offset, part, 0.0)
            strips[at] = strips[at] + part
        for c, strip in enumerate(strips):
            unsorted[q, c] = strip
            for k in range(srcs * planes):
                sorted_rows[q, c, k * points * parts:(k + 1) * points * parts] = unsorted[
                    q, c, pl.ds(k, points * parts, srcs * planes), :]
            for s in range(srcs):
                filt_out[s, q * share:(q + 1) * share, c * lanes:(c + 1) * lanes] = sorted_rows[
                    q, c, s * share:(s + 1) * share].astype(jnp.bfloat16)
    plane = lax.broadcasted_iota(jnp.int32, load_out.shape, 0)
    spread_load = jnp.zeros(load_out.shape, jnp.float32)
    for k in range(planes):
        spread_load = jnp.where(plane == k, quench_ref[k], spread_load)
    load_out[...] = spread_load

    greeted = srcs - 1 + jnp.where(has_above, 1, 0) + jnp.where(has_below, 1, 0)
    pl.semaphore_wait(barrier, greeted)

    def to_above():
        return pltpu.make_async_remote_copy(
            mask_ref, below, mask_send.at[0], mask_recv.at[0],
            device_id=(tile - 1, src), device_id_type=MESH)

    def to_below():
        return pltpu.make_async_remote_copy(
            mask_ref, above, mask_send.at[1], mask_recv.at[1],
            device_id=(tile + 1, src), device_id_type=MESH)

    @pl.when(has_above)
    def _():
        to_above().start()

    @pl.when(has_below)
    def _():
        to_below().start()

    filt_copies = []
    load_copies = []
    for at, peer in enumerate(peers):
        copy = pltpu.make_async_remote_copy(
            filt_out.at[peer], filters.at[src], filt_send.at[at], filt_recv.at[at],
            device_id=(tile, peer), device_id_type=MESH)
        copy.start()
        filt_copies.append(copy)
        copy = pltpu.make_async_remote_copy(
            load_out, loads.at[src], load_send.at[at], load_recv.at[at],
            device_id=(tile, peer), device_id_type=MESH)
        copy.start()
        load_copies.append(copy)
    filters[src] = filt_out[src]
    loads[src] = load_out[...]
    shifted[...] = jnp.zeros_like(shifted)

    @pl.when(jnp.logical_not(has_above))
    def _():
        above[...] = jnp.zeros_like(above)

    @pl.when(jnp.logical_not(has_below))
    def _():
        below[...] = jnp.zeros_like(below)

    @pl.when(has_above)
    def _():
        to_above().wait_send()
        to_below().wait_recv()

    @pl.when(has_below)
    def _():
        to_below().wait_send()
        to_above().wait_recv()

    image = jnp.concatenate([above[...], mask_ref[...], below[...]], axis=0).astype(jnp.float32)
    ring = jnp.concatenate([image, jnp.zeros((image.shape[0], 128), jnp.float32)], axis=1)
    length = cols + 128
    for b in range(side):
        moved = pltpu.roll(ring, (rim - b) % length, 1)[:, :cols]
        for c in range(cols // 128):
            shifted[c, pl.ds(b, image.shape[0], SLAB), :] = moved[:, c * 128:(c + 1) * 128]

    for g in range(tall // GROUP):
        for c in range(cols // 128):
            patches[g, :, c * 128:(c + 1) * 128] = shifted[
                c, g * GROUP * SLAB:g * GROUP * SLAB + DEEP, :].astype(jnp.bfloat16)
    light[...] = jnp.zeros_like(light)

    place = lax.broadcasted_iota(jnp.int32, (2 * share, WIRE), 1)
    ours = lax.broadcasted_iota(jnp.int32, (share, cols), 0) // (points * parts)
    for step in range(srcs):
        if step:
            filt_copies[step - 1].wait_recv()
        held = filters[lax.rem(src + srcs - step, srcs)].astype(jnp.float32)
        weights = jnp.sum(jnp.where(place == WIRE - 1, held, 0.0), axis=1, keepdims=True)[:share]
        held = jnp.where(place < side * SLAB, held, 0.0)
        held = jnp.concatenate([held, jnp.zeros((2 * share, DEEP - WIRE), jnp.float32)], axis=1)
        for r in range(GROUP):
            moved = pltpu.roll(held, r * SLAB, 1) if r else held
            taps[r * 2 * share:(r + 1) * 2 * share] = moved.astype(jnp.bfloat16)

        def one_group(g, carry):
            field = jnp.dot(taps[...], patches[g], preferred_element_type=jnp.float32)
            square = (field * field).reshape(GROUP, 2, share, cols)
            power = (square[:, 0] + square[:, 1]) * weights
            start = pl.multiple_of(g * GROUP, GROUP)
            for k in range(planes):
                own = jnp.where(ours == k, power, 0.0)
                light[k, pl.ds(start, GROUP), :] += jnp.sum(own, axis=1)
            return carry

        lax.fori_loop(0, tall // GROUP, one_group, 0)
    for copy in load_copies:
        copy.wait()
    for copy in filt_copies:
        copy.wait_send()

    edge = lax.broadcasted_iota(jnp.int32, (GROUP, 128), 1)
    none = jnp.zeros((GROUP, 128), jnp.float32)
    rims = [none] * srcs
    for k in range(planes):
        exposed = light[k] * (dill_ref[k] * scale)
        for s in range(srcs):
            light_out[s, k] = exposed[:, s * block:(s + 1) * block].astype(jnp.bfloat16)
            for g in range(tall // GROUP):
                rows8 = exposed[g * GROUP:(g + 1) * GROUP]
                right = rows8[:, (s + 1) * block:(s + 1) * block + 128] if s < srcs - 1 else none
                left = rows8[:, s * block - 128:s * block] if s else none
                picked = jnp.where(edge < halo, right, jnp.where(edge >= 128 - halo, left, 0.0))
                shift = 2 * halo * (k * (tall // GROUP) + g)
                rims[s] = rims[s] + (pltpu.roll(picked, shift, 1) if shift else picked)
    for s in range(srcs):
        rim_out[s] = rims[s]
    copies = []
    for at, peer in enumerate(peers):
        copy = pltpu.make_async_remote_copy(
            light_out.at[peer], light_in.at[src], light_send.at[at], light_recv.at[at],
            device_id=(tile, peer), device_id_type=MESH)
        copy.start()
        copies.append(copy)
        copy = pltpu.make_async_remote_copy(
            rim_out.at[peer], rim_in.at[src], rim_send.at[at], rim_recv.at[at],
            device_id=(tile, peer), device_id_type=MESH)
        copy.start()
        copies.append(copy)
    light_in[src] = light_out[src]
    rim_in[src] = rim_out[src]
    row = lax.broadcasted_iota(jnp.int32, (tall, wide), 0) + (tile * rows - halo)
    col = lax.broadcasted_iota(jnp.int32, (tall, wide), 1)
    col = src * block + jnp.where(col < block + 64, col, col - wide)
    inside = (row >= 0) & (row < tiles * rows) & (col >= 0) & (col < cols)
    inside = jnp.where(inside, 1.0, 0.0)
    for copy in copies:
        copy.wait()

    depth = srcs * planes
    for k in range(depth):
        sent = rim_in[k // planes]
        rim = []
        for g in range(tall // GROUP):
            shift = 2 * halo * (k % planes * (tall // GROUP) + g)
            rim.append(pltpu.roll(sent, 128 - shift, 1) if shift else sent)
        exposed = jnp.concatenate(
            [light_in[k // planes, k % planes].astype(jnp.float32), jnp.concatenate(rim, axis=0)], axis=1)
        acid[0, k] = (1.0 - jnp.exp(-exposed)) * inside
        quench[0, k] = loads[k // planes, k % planes:k % planes + 1, 0:1] * inside
        dose[k] = jnp.zeros((rows, block), jnp.float32)

    def blend(centre, sides, vertical, lateral_rate, vertical_rate):
        stay = 1.0 - 4.0 * lateral_rate - 2.0 * vertical_rate
        return stay * centre + lateral_rate * sides + vertical_rate * vertical

    def spread(held, now, k, lateral_rate, vertical_rate):
        centre = held[now, k]
        sides = (
            pltpu.roll(centre, 1, 0) + pltpu.roll(centre, tall - 1, 0)
            + pltpu.roll(centre, 1, 1) + pltpu.roll(centre, wide - 1, 1)
        )
        vertical = held[now, min(k + 1, depth - 1)] + held[now, max(k - 1, 0)]
        return centre, blend(centre, sides, vertical, lateral_rate, vertical_rate)

    def one_step(now):
        for k in range(depth):
            a, a_next = spread(acid, now, k, acid_lateral, acid_vertical)
            q, q_next = spread(quench, now, k, quench_lateral, quench_vertical)
            reacted = react_rate * a * q
            a_next = (a_next - reacted) * inside
            acid[1 - now, k] = a_next
            quench[1 - now, k] = (q_next - reacted) * inside
            dose[k] = dose[k] + a_next[halo:halo + rows, :block]

    def two_steps(pair, carry):
        one_step(0)
        one_step(1)
        return carry

    lax.fori_loop(0, STEPS // 2 - 1, two_steps, 0)
    one_step(0)

    def final_copy(s, slot):
        return pltpu.make_async_remote_copy(
            final_out.at[s], final_in.at[slot], final_send.at[s], final_recv.at[slot],
            device_id=(tile, s), device_id_type=MESH)

    own = slice(halo, halo + rows)
    for s in range(srcs):
        for k in range(s * planes, (s + 1) * planes):
            strip = acid[1, k, own]
            centre = strip[:, :block]
            sides = (
                acid[1, k, halo - 1:halo + rows - 1, :block] + acid[1, k, halo + 1:halo + rows + 1, :block]
                + pltpu.roll(strip, 1, 1)[:, :block] + pltpu.roll(strip, wide - 1, 1)[:, :block]
            )
            vertical = acid[1, min(k + 1, depth - 1), own, :block] + acid[1, max(k - 1, 0), own, :block]
            reacted = react_rate * centre * quench[1, k, own, :block]
            a_next = blend(centre, sides, vertical, acid_lateral, acid_vertical) - reacted
            final_out[s, 0, k % planes] = a_next
            final_out[s, 1, k % planes] = jnp.exp(-deprotect_rate * (dose[k] + a_next))

        @pl.when(src != s)
        def _():
            final_copy(s, src).start()

        @pl.when(src == s)
        def _():
            final_in[s] = final_out[s]

    for s in range(srcs):
        @pl.when(src != s)
        def _():
            final_copy(s, src).wait_send()
            final_copy(s, s).wait_recv()

    for s in range(srcs):
        acid_ref[:, :, s * block:(s + 1) * block] = final_in[s, 0]
        inhib_ref[:, :, s * block:(s + 1) * block] = final_in[s, 1]


def shards(mask_tiles, kernels, source_weight, dill_rate, quencher_load):
    tiles, srcs = lax.axis_size("tile"), lax.axis_size("src")
    rows, cols = mask_tiles.shape
    planes = dill_rate.shape[0]
    points, parts, depth, quad, side, _ = kernels.shape
    share = planes * points * parts
    raw = kernels.transpose(0, 1, 2, 4, 3, 5).reshape(-1, side)
    dims = (tiles, srcs, rows, cols, side, planes, 1.0 / (24.0 * points * srcs))
    tall = rows + 2 * STEPS
    block = cols // srcs
    wide = block + 128
    depth_all = srcs * planes
    f32 = jnp.float32
    image_rows = 3 * rows
    deep_rows = max(image_rows * SLAB, (tall - GROUP) * SLAB + DEEP)
    out = jax.ShapeDtypeStruct((planes, rows, cols), f32)
    vmem = pl.BlockSpec(memory_space=pltpu.VMEM)
    smem = pl.BlockSpec(memory_space=pltpu.SMEM)
    dma = pltpu.SemaphoreType.DMA
    return pl.pallas_call(
        functools.partial(kernel, dims),
        out_shape=(out, out),
        in_specs=[vmem, vmem, smem, smem, smem],
        out_specs=(vmem, vmem),
        scratch_shapes=[
            pltpu.VMEM((rows, cols), jnp.int32),
            pltpu.VMEM((rows, cols), jnp.int32),
            pltpu.VMEM((raw.shape[0], 128), f32),
            pltpu.VMEM((2, WIRE // 128, srcs * share, 128), f32),
            pltpu.VMEM((2, WIRE // 128, srcs * share, 128), f32),
            pltpu.VMEM((srcs, 2 * share, WIRE), jnp.bfloat16),
            pltpu.VMEM((8, 128), f32),
            pltpu.VMEM((srcs, 2 * share, WIRE), jnp.bfloat16),
            pltpu.VMEM((srcs, 8, 128), f32),
            pltpu.VMEM((cols // 128, deep_rows, 128), f32),
            pltpu.VMEM((tall // GROUP, DEEP, cols), jnp.bfloat16),
            pltpu.VMEM((GROUP * 2 * share, DEEP), jnp.bfloat16),
            pltpu.VMEM((planes, tall, cols), f32),
            pltpu.VMEM((srcs, planes, tall, block), jnp.bfloat16),
            pltpu.VMEM((srcs, planes, tall, block), jnp.bfloat16),
            pltpu.VMEM((srcs, GROUP, 128), f32),
            pltpu.VMEM((srcs, GROUP, 128), f32),
            pltpu.VMEM((2, depth_all, tall, wide), f32),
            pltpu.VMEM((2, depth_all, tall, wide), f32),
            pltpu.VMEM((depth_all, rows, block), f32),
            pltpu.VMEM((srcs, 2, planes, rows, block), f32),
            pltpu.VMEM((srcs, 2, planes, rows, block), f32),
            dma((2,)), dma((2,)),
            dma((srcs - 1,)), dma((srcs - 1,)),
            dma((srcs - 1,)), dma((srcs - 1,)),
            dma((srcs - 1,)), dma((srcs - 1,)),
            dma((srcs - 1,)), dma((srcs - 1,)),
            dma((srcs,)), dma((srcs,)),
        ],
        compiler_params=pltpu.CompilerParams(
            collective_id=0, has_side_effects=True, vmem_limit_bytes=40 * 1024 * 1024
        ),
    )(mask_tiles, raw, source_weight, dill_rate, quencher_load)


def solution(mesh):
    in_specs = (
        P("tile", None),
        P("src", None, None, None, None, None),
        P("src"),
        P("src"),
        P("src"),
    )
    out_specs = (P("src", "tile", None), P("src", "tile", None))
    return jax.shard_map(shards, mesh=mesh, in_specs=in_specs, out_specs=out_specs, check_vma=False)
```

```python
import functools

import jax
import jax.numpy as jnp
from jax import lax
from jax.experimental import pallas as pl
from jax.experimental.pallas import tpu as pltpu
from jax.sharding import PartitionSpec as P

STEPS = 8
SLAB = 21
DEEP = 512
WIRE = 384
GROUP = 8

acid_lateral = 0.15
acid_vertical = 0.12
quench_lateral = 0.05
quench_vertical = 0.04
react_rate = 0.3
deprotect_rate = 0.25

MESH = pl.DeviceIdType.MESH


def kernel(
    dims,
    mask_hbm, raw_hbm, pupil_hbm, dill_hbm, quench_hbm, out_hbm,
    mask_ref, raw_ref, pupil_ref, dill_ref, quench_ref, above, below, raw, unsorted, sorted_rows, filt_out, load_out, filters, loads, shifted, patches, taps,
    light, light_out, light_in, rim_out, rim_in,
    acid, quench, dose, final_out, final_in,
    here_sem, out_sem, mask_send, mask_recv, filt_send, filt_recv, load_send, load_recv,
    light_send, light_recv, rim_send, rim_recv, final_send, final_recv,
):
    tiles, srcs, rows, cols, side, planes, scale = dims
    rim = side // 2
    halo = STEPS
    tall = rows + 2 * halo
    block = cols // srcs
    wide = block + 128
    local = [
        pltpu.make_async_copy(there, here, here_sem.at[at])
        for at, (there, here) in enumerate((
            (raw_hbm, raw_ref), (pupil_hbm, pupil_ref), (quench_hbm, quench_ref),
            (mask_hbm, mask_ref), (dill_hbm, dill_ref)))
    ]
    for copy in local:
        copy.start()
    tile = lax.axis_index("tile")
    src = lax.axis_index("src")
    has_above = tile > 0
    has_below = tile < tiles - 1

    barrier = pltpu.get_barrier_semaphore()
    peers = [lax.rem(src + step, srcs) for step in range(1, srcs)]
    for peer in peers:
        pl.semaphore_signal(barrier, inc=1, device_id=(tile, peer), device_id_type=MESH)

    @pl.when(has_above)
    def _():
        pl.semaphore_signal(barrier, inc=1, device_id=(tile - 1, src), device_id_type=MESH)

    @pl.when(has_below)
    def _():
        pl.semaphore_signal(barrier, inc=1, device_id=(tile + 1, src), device_id_type=MESH)

    raw[...] = jnp.zeros_like(raw)
    shifted[...] = jnp.zeros_like(shifted)
    for copy in local:
        copy.wait()
    lanes = 128
    points, parts = pupil_ref.shape[0], raw_ref.shape[0] // (2 * side * srcs * planes * pupil_ref.shape[0])
    channels = srcs * planes * points * parts
    share = planes * points * parts
    lane = lax.broadcasted_iota(jnp.int32, (channels, lanes), 1)
    point = lax.broadcasted_iota(jnp.int32, (channels, lanes), 0) // (srcs * planes * parts)
    weight = jnp.zeros((channels, lanes), jnp.float32)
    for p in range(points):
        weight = jnp.where(point == p, pupil_ref[p].astype(jnp.float32), weight)
    weight = jnp.where(lane == lanes - 1, weight, 0.0)
    def widen(at, carry):
        here = pl.ds(pl.multiple_of(at * channels, channels), channels)
        raw[here, :side] = raw_ref[here, :].astype(jnp.float32)
        return carry

    lax.fori_loop(0, 2 * side, widen, 0)
    for q in range(2):
        strips = [jnp.zeros((channels, lanes), jnp.float32) for _ in range(WIRE // lanes)]
        strips[-1] = weight
        for a in range(side):
            part = raw[pl.ds(2 * a + q, channels, 2 * side), :]
            at, offset = divmod(a * SLAB, lanes)
            if offset:
                part = pltpu.roll(part, offset, 1)
            if offset + side > lanes:
                strips[at + 1] = strips[at + 1] + jnp.where(lane < offset, part, 0.0)
                part = jnp.where(lane >= offset, part, 0.0)
            strips[at] = strips[at] + part
        for c, strip in enumerate(strips):
            unsorted[q, c] = strip
            for k in range(srcs * planes):
                sorted_rows[q, c, k * points * parts:(k + 1) * points * parts] = unsorted[
                    q, c, pl.ds(k, points * parts, srcs * planes), :]
            for s in range(srcs):
                filt_out[s, q * share:(q + 1) * share, c * lanes:(c + 1) * lanes] = sorted_rows[
                    q, c, s * share:(s + 1) * share].astype(jnp.bfloat16)
    plane = lax.broadcasted_iota(jnp.int32, load_out.shape, 0)
    spread_load = jnp.zeros(load_out.shape, jnp.float32)
    for k in range(planes):
        spread_load = jnp.where(plane == k, quench_ref[k], spread_load)
    load_out[...] = spread_load

    greeted = srcs - 1 + jnp.where(has_above, 1, 0) + jnp.where(has_below, 1, 0)
    pl.semaphore_wait(barrier, greeted)

    def to_above():
        return pltpu.make_async_remote_copy(
            mask_ref, below, mask_send.at[0], mask_recv.at[0],
            device_id=(tile - 1, src), device_id_type=MESH)

    def to_below():
        return pltpu.make_async_remote_copy(
            mask_ref, above, mask_send.at[1], mask_recv.at[1],
            device_id=(tile + 1, src), device_id_type=MESH)

    @pl.when(has_above)
    def _():
        to_above().start()

    @pl.when(has_below)
    def _():
        to_below().start()

    filt_copies = []
    load_copies = []
    for at, peer in enumerate(peers):
        copy = pltpu.make_async_remote_copy(
            filt_out.at[peer], filters.at[src], filt_send.at[at], filt_recv.at[at],
            device_id=(tile, peer), device_id_type=MESH)
        copy.start()
        filt_copies.append(copy)
        copy = pltpu.make_async_remote_copy(
            load_out, loads.at[src], load_send.at[at], load_recv.at[at],
            device_id=(tile, peer), device_id_type=MESH)
        copy.start()
        load_copies.append(copy)
    filters[src] = filt_out[src]
    loads[src] = load_out[...]

    @pl.when(jnp.logical_not(has_above))
    def _():
        above[...] = jnp.zeros_like(above)

    @pl.when(jnp.logical_not(has_below))
    def _():
        below[...] = jnp.zeros_like(below)

    @pl.when(has_above)
    def _():
        to_above().wait_send()
        to_below().wait_recv()

    @pl.when(has_below)
    def _():
        to_below().wait_send()
        to_above().wait_recv()

    image = jnp.concatenate([above[...], mask_ref[...], below[...]], axis=0).astype(jnp.float32)
    ring = jnp.concatenate([image, jnp.zeros((image.shape[0], 128), jnp.float32)], axis=1)
    length = cols + 128
    for b in range(side):
        moved = pltpu.roll(ring, (rim - b) % length, 1)[:, :cols]
        for c in range(cols // 128):
            shifted[c, pl.ds(b, image.shape[0], SLAB), :] = moved[:, c * 128:(c + 1) * 128]

    for g in range(tall // GROUP):
        for c in range(cols // 128):
            patches[g, :, c * 128:(c + 1) * 128] = shifted[
                c, g * GROUP * SLAB:g * GROUP * SLAB + DEEP, :].astype(jnp.bfloat16)
    light[...] = jnp.zeros_like(light)

    place = lax.broadcasted_iota(jnp.int32, (2 * share, WIRE), 1)
    ours = lax.broadcasted_iota(jnp.int32, (share, cols), 0) // (points * parts)
    for step in range(srcs):
        if step:
            filt_copies[step - 1].wait_recv()
        held = filters[lax.rem(src + srcs - step, srcs)].astype(jnp.float32)
        weights = jnp.sum(jnp.where(place == WIRE - 1, held, 0.0), axis=1, keepdims=True)[:share]
        held = jnp.where(place < side * SLAB, held, 0.0)
        held = jnp.concatenate([held, jnp.zeros((2 * share, DEEP - WIRE), jnp.float32)], axis=1)
        for r in range(GROUP):
            moved = pltpu.roll(held, r * SLAB, 1) if r else held
            taps[r * 2 * share:(r + 1) * 2 * share] = moved.astype(jnp.bfloat16)

        def one_group(g, carry):
            field = jnp.dot(taps[...], patches[g], preferred_element_type=jnp.float32)
            square = (field * field).reshape(GROUP, 2, share, cols)
            power = (square[:, 0] + square[:, 1]) * weights
            start = pl.multiple_of(g * GROUP, GROUP)
            for k in range(planes):
                own = jnp.where(ours == k, power, 0.0)
                light[k, pl.ds(start, GROUP), :] += jnp.sum(own, axis=1)
            return carry

        lax.fori_loop(0, tall // GROUP, one_group, 0)
    for copy in load_copies:
        copy.wait()
    for copy in filt_copies:
        copy.wait_send()

    edge = lax.broadcasted_iota(jnp.int32, (GROUP, 128), 1)
    none = jnp.zeros((GROUP, 128), jnp.float32)
    rims = [none] * srcs
    for k in range(planes):
        exposed = light[k] * (dill_ref[k] * scale)
        for s in range(srcs):
            light_out[s, k] = exposed[:, s * block:(s + 1) * block].astype(jnp.bfloat16)
            for g in range(tall // GROUP):
                rows8 = exposed[g * GROUP:(g + 1) * GROUP]
                right = rows8[:, (s + 1) * block:(s + 1) * block + 128] if s < srcs - 1 else none
                left = rows8[:, s * block - 128:s * block] if s else none
                picked = jnp.where(edge < halo, right, jnp.where(edge >= 128 - halo, left, 0.0))
                shift = 2 * halo * (k * (tall // GROUP) + g)
                rims[s] = rims[s] + (pltpu.roll(picked, shift, 1) if shift else picked)
    for s in range(srcs):
        rim_out[s] = rims[s]
    copies = []
    for at, peer in enumerate(peers):
        copy = pltpu.make_async_remote_copy(
            light_out.at[peer], light_in.at[src], light_send.at[at], light_recv.at[at],
            device_id=(tile, peer), device_id_type=MESH)
        copy.start()
        copies.append(copy)
        copy = pltpu.make_async_remote_copy(
            rim_out.at[peer], rim_in.at[src], rim_send.at[at], rim_recv.at[at],
            device_id=(tile, peer), device_id_type=MESH)
        copy.start()
        copies.append(copy)
    light_in[src] = light_out[src]
    rim_in[src] = rim_out[src]
    row = lax.broadcasted_iota(jnp.int32, (tall, wide), 0) + (tile * rows - halo)
    col = lax.broadcasted_iota(jnp.int32, (tall, wide), 1)
    col = src * block + jnp.where(col < block + 64, col, col - wide)
    inside = (row >= 0) & (row < tiles * rows) & (col >= 0) & (col < cols)
    inside = jnp.where(inside, 1.0, 0.0)
    for copy in copies:
        copy.wait()

    depth = srcs * planes
    for k in range(depth):
        sent = rim_in[k // planes]
        rim = []
        for g in range(tall // GROUP):
            shift = 2 * halo * (k % planes * (tall // GROUP) + g)
            rim.append(pltpu.roll(sent, 128 - shift, 1) if shift else sent)
        exposed = jnp.concatenate(
            [light_in[k // planes, k % planes].astype(jnp.float32), jnp.concatenate(rim, axis=0)], axis=1)
        acid[0, k] = (1.0 - jnp.exp(-exposed)) * inside
        quench[0, k] = loads[k // planes, k % planes:k % planes + 1, 0:1] * inside
        dose[k] = jnp.zeros((rows, block), jnp.float32)

    def blend(centre, sides, vertical, lateral_rate, vertical_rate):
        stay = 1.0 - 4.0 * lateral_rate - 2.0 * vertical_rate
        return stay * centre + lateral_rate * sides + vertical_rate * vertical

    def spread(held, now, k, lateral_rate, vertical_rate):
        centre = held[now, k]
        sides = (
            pltpu.roll(centre, 1, 0) + pltpu.roll(centre, tall - 1, 0)
            + pltpu.roll(centre, 1, 1) + pltpu.roll(centre, wide - 1, 1)
        )
        vertical = held[now, min(k + 1, depth - 1)] + held[now, max(k - 1, 0)]
        return centre, blend(centre, sides, vertical, lateral_rate, vertical_rate)

    def one_step(now):
        for k in range(depth):
            a, a_next = spread(acid, now, k, acid_lateral, acid_vertical)
            q, q_next = spread(quench, now, k, quench_lateral, quench_vertical)
            reacted = react_rate * a * q
            a_next = (a_next - reacted) * inside
            acid[1 - now, k] = a_next
            quench[1 - now, k] = (q_next - reacted) * inside
            dose[k] = dose[k] + a_next[halo:halo + rows, :block]

    def two_steps(pair, carry):
        one_step(0)
        one_step(1)
        return carry

    lax.fori_loop(0, STEPS // 2 - 1, two_steps, 0)
    one_step(0)

    def final_copy(s, slot):
        return pltpu.make_async_remote_copy(
            final_out.at[s], final_in.at[slot], final_send.at[s], final_recv.at[slot],
            device_id=(tile, s), device_id_type=MESH)

    own = slice(halo, halo + rows)
    for s in range(srcs):
        for k in range(s * planes, (s + 1) * planes):
            strip = acid[1, k, own]
            centre = strip[:, :block]
            sides = (
                acid[1, k, halo - 1:halo + rows - 1, :block] + acid[1, k, halo + 1:halo + rows + 1, :block]
                + pltpu.roll(strip, 1, 1)[:, :block] + pltpu.roll(strip, wide - 1, 1)[:, :block]
            )
            vertical = acid[1, min(k + 1, depth - 1), own, :block] + acid[1, max(k - 1, 0), own, :block]
            reacted = react_rate * centre * quench[1, k, own, :block]
            a_next = blend(centre, sides, vertical, acid_lateral, acid_vertical) - reacted
            final_out[s, 0, k % planes] = a_next
            final_out[s, 1, k % planes] = dose[k] + a_next

        @pl.when(src != s)
        def _():
            final_copy(s, src).start()

        @pl.when(src == s)
        def _():
            final_in[s] = final_out[s]

    def place_copy(s):
        return pltpu.make_async_copy(
            final_in.at[s], out_hbm.at[:, :, :, s * block:(s + 1) * block], out_sem.at[s])

    for s in range(srcs):
        @pl.when(src != s)
        def _():
            final_copy(s, s).wait_recv()

        place_copy(s).start()
    for s in range(srcs):
        place_copy(s).wait()

        @pl.when(src != s)
        def _():
            final_copy(s, src).wait_send()


def shards(mask_tiles, kernels, source_weight, dill_rate, quencher_load):
    tiles, srcs = lax.axis_size("tile"), lax.axis_size("src")
    rows, cols = mask_tiles.shape
    planes = dill_rate.shape[0]
    points, parts, depth, quad, side, _ = kernels.shape
    share = planes * points * parts
    raw = kernels.transpose(0, 1, 2, 4, 3, 5).reshape(-1, side)
    dims = (tiles, srcs, rows, cols, side, planes, 1.0 / (24.0 * points * srcs))
    tall = rows + 2 * STEPS
    block = cols // srcs
    wide = block + 128
    depth_all = srcs * planes
    f32 = jnp.float32
    image_rows = 3 * rows
    deep_rows = max(image_rows * SLAB, (tall - GROUP) * SLAB + DEEP)
    out = jax.ShapeDtypeStruct((2, planes, rows, cols), f32)
    dma = pltpu.SemaphoreType.DMA
    result = pl.pallas_call(
        functools.partial(kernel, dims),
        out_shape=out,
        in_specs=[pl.BlockSpec(memory_space=pltpu.HBM)] * 5,
        out_specs=pl.BlockSpec(memory_space=pl.ANY),
        scratch_shapes=[
            pltpu.VMEM(mask_tiles.shape, jnp.int32),
            pltpu.VMEM(raw.shape, jnp.bfloat16),
            pltpu.SMEM(source_weight.shape, jnp.int32),
            pltpu.SMEM(dill_rate.shape, f32),
            pltpu.SMEM(quencher_load.shape, f32),
            pltpu.VMEM((rows, cols), jnp.int32),
            pltpu.VMEM((rows, cols), jnp.int32),
            pltpu.VMEM((raw.shape[0], 128), f32),
            pltpu.VMEM((2, WIRE // 128, srcs * share, 128), f32),
            pltpu.VMEM((2, WIRE // 128, srcs * share, 128), f32),
            pltpu.VMEM((srcs, 2 * share, WIRE), jnp.bfloat16),
            pltpu.VMEM((8, 128), f32),
            pltpu.VMEM((srcs, 2 * share, WIRE), jnp.bfloat16),
            pltpu.VMEM((srcs, 8, 128), f32),
            pltpu.VMEM((cols // 128, deep_rows, 128), f32),
            pltpu.VMEM((tall // GROUP, DEEP, cols), jnp.bfloat16),
            pltpu.VMEM((GROUP * 2 * share, DEEP), jnp.bfloat16),
            pltpu.VMEM((planes, tall, cols), f32),
            pltpu.VMEM((srcs, planes, tall, block), jnp.bfloat16),
            pltpu.VMEM((srcs, planes, tall, block), jnp.bfloat16),
            pltpu.VMEM((srcs, GROUP, 128), f32),
            pltpu.VMEM((srcs, GROUP, 128), f32),
            pltpu.VMEM((2, depth_all, tall, wide), f32),
            pltpu.VMEM((2, depth_all, tall, wide), f32),
            pltpu.VMEM((depth_all, rows, block), f32),
            pltpu.VMEM((srcs, 2, planes, rows, block), f32),
            pltpu.VMEM((srcs, 2, planes, rows, block), f32),
            dma((5,)), dma((srcs,)), dma((2,)), dma((2,)),
            dma((srcs - 1,)), dma((srcs - 1,)),
            dma((srcs - 1,)), dma((srcs - 1,)),
            dma((srcs - 1,)), dma((srcs - 1,)),
            dma((srcs - 1,)), dma((srcs - 1,)),
            dma((srcs,)), dma((srcs,)),
        ],
        compiler_params=pltpu.CompilerParams(
            collective_id=0, has_side_effects=True, vmem_limit_bytes=60 * 1024 * 1024
        ),
    )(mask_tiles, raw, source_weight, dill_rate, quencher_load)
    return result[0], jnp.exp(-deprotect_rate * result[1])


def solution(mesh):
    in_specs = (
        P("tile", None),
        P("src", None, None, None, None, None),
        P("src"),
        P("src"),
        P("src"),
    )
    out_specs = (P("src", "tile", None), P("src", "tile", None))
    return jax.shard_map(shards, mesh=mesh, in_specs=in_specs, out_specs=out_specs, check_vma=False)
```

```python
import functools

import jax
import jax.numpy as jnp
from jax import lax
from jax.experimental import pallas as pl
from jax.experimental.pallas import tpu as pltpu
from jax.sharding import PartitionSpec as P

STEPS = 8
SLAB = 21
DEEP = 512
WIRE = 384
GROUP = 8

acid_lateral = 0.15
acid_vertical = 0.12
quench_lateral = 0.05
quench_vertical = 0.04
react_rate = 0.3
deprotect_rate = 0.25

MESH = pl.DeviceIdType.MESH


def kernel(
    dims,
    mask_hbm, raw_hbm, pupil_hbm, dill_hbm, quench_hbm, out_hbm,
    mask_ref, raw_ref, pupil_ref, dill_ref, quench_ref, above, below, raw, unsorted, sorted_rows, filt_out, load_out, filters, loads, shifted, patches, taps,
    light, light_out, light_in, rim_out, rim_in,
    acid, quench, dose, final_out, final_in,
    here_sem, out_sem, mask_send, mask_recv, filt_send, filt_recv, load_send, load_recv,
    light_send, light_recv, rim_send, rim_recv, final_send, final_recv,
):
    tiles, srcs, rows, cols, side, planes, scale = dims
    rim = side // 2
    halo = STEPS
    tall = rows + 2 * halo
    block = cols // srcs
    wide = block + 128
    local = [
        pltpu.make_async_copy(there, here, here_sem.at[at])
        for at, (there, here) in enumerate((
            (raw_hbm, raw_ref), (pupil_hbm, pupil_ref), (quench_hbm, quench_ref),
            (mask_hbm, mask_ref), (dill_hbm, dill_ref)))
    ]
    for copy in local:
        copy.start()
    tile = lax.axis_index("tile")
    src = lax.axis_index("src")
    has_above = tile > 0
    has_below = tile < tiles - 1

    barrier = pltpu.get_barrier_semaphore()
    peers = [lax.rem(src + step, srcs) for step in range(1, srcs)]
    for peer in peers:
        pl.semaphore_signal(barrier, inc=1, device_id=(tile, peer), device_id_type=MESH)

    @pl.when(has_above)
    def _():
        pl.semaphore_signal(barrier, inc=1, device_id=(tile - 1, src), device_id_type=MESH)

    @pl.when(has_below)
    def _():
        pl.semaphore_signal(barrier, inc=1, device_id=(tile + 1, src), device_id_type=MESH)

    raw[...] = jnp.zeros_like(raw)
    shifted[...] = jnp.zeros_like(shifted)
    for copy in local:
        copy.wait()
    lanes = 128
    points, parts = pupil_ref.shape[0], raw_ref.shape[0] // (2 * side * srcs * planes * pupil_ref.shape[0])
    channels = srcs * planes * points * parts
    share = planes * points * parts
    lane = lax.broadcasted_iota(jnp.int32, (channels, lanes), 1)
    point = lax.broadcasted_iota(jnp.int32, (channels, lanes), 0) // (srcs * planes * parts)
    weight = jnp.zeros((channels, lanes), jnp.float32)
    for p in range(points):
        weight = jnp.where(point == p, pupil_ref[p].astype(jnp.float32), weight)
    weight = jnp.where(lane == lanes - 1, weight, 0.0)
    def widen(at, carry):
        here = pl.ds(pl.multiple_of(at * channels, channels), channels)
        raw[here, :side] = raw_ref[here, :].astype(jnp.float32)
        return carry

    lax.fori_loop(0, 2 * side, widen, 0)
    for q in range(2):
        strips = [jnp.zeros((channels, lanes), jnp.float32) for _ in range(WIRE // lanes)]
        strips[-1] = weight
        for a in range(side):
            part = raw[pl.ds(2 * a + q, channels, 2 * side), :]
            at, offset = divmod(a * SLAB, lanes)
            if offset:
                part = pltpu.roll(part, offset, 1)
            if offset + side > lanes:
                strips[at + 1] = strips[at + 1] + jnp.where(lane < offset, part, 0.0)
                part = jnp.where(lane >= offset, part, 0.0)
            strips[at] = strips[at] + part
        for c, strip in enumerate(strips):
            unsorted[q, c] = strip
            for k in range(srcs * planes):
                sorted_rows[q, c, k * points * parts:(k + 1) * points * parts] = unsorted[
                    q, c, pl.ds(k, points * parts, srcs * planes), :]
            for s in range(srcs):
                filt_out[s, q * share:(q + 1) * share, c * lanes:(c + 1) * lanes] = sorted_rows[
                    q, c, s * share:(s + 1) * share].astype(jnp.bfloat16)
    plane = lax.broadcasted_iota(jnp.int32, load_out.shape, 0)
    spread_load = jnp.zeros(load_out.shape, jnp.float32)
    for k in range(planes):
        spread_load = jnp.where(plane == k, quench_ref[k], spread_load)
    load_out[...] = spread_load

    greeted = srcs - 1 + jnp.where(has_above, 1, 0) + jnp.where(has_below, 1, 0)
    pl.semaphore_wait(barrier, greeted)

    def to_above():
        return pltpu.make_async_remote_copy(
            mask_ref, below, mask_send.at[0], mask_recv.at[0],
            device_id=(tile - 1, src), device_id_type=MESH)

    def to_below():
        return pltpu.make_async_remote_copy(
            mask_ref, above, mask_send.at[1], mask_recv.at[1],
            device_id=(tile + 1, src), device_id_type=MESH)

    @pl.when(has_above)
    def _():
        to_above().start()

    @pl.when(has_below)
    def _():
        to_below().start()

    filt_copies = []
    load_copies = []
    for at, peer in enumerate(peers):
        copy = pltpu.make_async_remote_copy(
            filt_out.at[peer], filters.at[src], filt_send.at[at], filt_recv.at[at],
            device_id=(tile, peer), device_id_type=MESH)
        copy.start()
        filt_copies.append(copy)
        copy = pltpu.make_async_remote_copy(
            load_out, loads.at[src], load_send.at[at], load_recv.at[at],
            device_id=(tile, peer), device_id_type=MESH)
        copy.start()
        load_copies.append(copy)
    filters[src] = filt_out[src]
    loads[src] = load_out[...]

    @pl.when(jnp.logical_not(has_above))
    def _():
        above[...] = jnp.zeros_like(above)

    @pl.when(jnp.logical_not(has_below))
    def _():
        below[...] = jnp.zeros_like(below)

    @pl.when(has_above)
    def _():
        to_above().wait_send()
        to_below().wait_recv()

    @pl.when(has_below)
    def _():
        to_below().wait_send()
        to_above().wait_recv()

    image = jnp.concatenate([above[...], mask_ref[...], below[...]], axis=0).astype(jnp.float32)
    ring = jnp.concatenate([image, jnp.zeros((image.shape[0], 128), jnp.float32)], axis=1)
    length = cols + 128
    for b in range(side):
        moved = pltpu.roll(ring, (rim - b) % length, 1)[:, :cols]
        for c in range(cols // 128):
            shifted[c, pl.ds(b, image.shape[0], SLAB), :] = moved[:, c * 128:(c + 1) * 128]

    for g in range(tall // GROUP):
        for c in range(cols // 128):
            patches[g, :, c * 128:(c + 1) * 128] = shifted[
                c, g * GROUP * SLAB:g * GROUP * SLAB + DEEP, :].astype(jnp.bfloat16)
    light[...] = jnp.zeros_like(light)

    half = tall // 2
    edge = lax.broadcasted_iota(jnp.int32, (GROUP, 128), 1)
    none = jnp.zeros((GROUP, 128), jnp.float32)
    rims = [none] * srcs
    copies = []

    def ship(h):
        for k in range(planes):
            exposed = light[k, h * half:(h + 1) * half] * (dill_ref[k] * scale)
            for s in range(srcs):
                light_out[h, s, k] = exposed[:, s * block:(s + 1) * block].astype(jnp.bfloat16)
                for g in range(half // GROUP):
                    rows8 = exposed[g * GROUP:(g + 1) * GROUP]
                    right = rows8[:, (s + 1) * block:(s + 1) * block + 128] if s < srcs - 1 else none
                    left = rows8[:, s * block - 128:s * block] if s else none
                    picked = jnp.where(edge < halo, right, jnp.where(edge >= 128 - halo, left, 0.0))
                    shift = 2 * halo * (k * (tall // GROUP) + h * (half // GROUP) + g)
                    rims[s] = rims[s] + (pltpu.roll(picked, shift, 1) if shift else picked)
        for at, peer in enumerate(peers):
            copy = pltpu.make_async_remote_copy(
                light_out.at[h, peer], light_in.at[h, src], light_send.at[h, at], light_recv.at[h, at],
                device_id=(tile, peer), device_id_type=MESH)
            copy.start()
            copies.append(copy)
        light_in[h, src] = light_out[h, src]

    place = lax.broadcasted_iota(jnp.int32, (2 * share, WIRE), 1)
    ours = lax.broadcasted_iota(jnp.int32, (share, cols), 0) // (points * parts)
    for step in range(srcs):
        if step:
            filt_copies[step - 1].wait_recv()
        held = filters[lax.rem(src + srcs - step, srcs)].astype(jnp.float32)
        weights = jnp.sum(jnp.where(place == WIRE - 1, held, 0.0), axis=1, keepdims=True)[:share]
        held = jnp.where(place < side * SLAB, held, 0.0)
        held = jnp.concatenate([held, jnp.zeros((2 * share, DEEP - WIRE), jnp.float32)], axis=1)
        for r in range(GROUP):
            moved = pltpu.roll(held, r * SLAB, 1) if r else held
            taps[r * 2 * share:(r + 1) * 2 * share] = moved.astype(jnp.bfloat16)

        for g in range(tall // GROUP):
            field = jnp.dot(taps[...], patches[g], preferred_element_type=jnp.float32)
            square = (field * field).reshape(GROUP, 2, share, cols)
            power = (square[:, 0] + square[:, 1]) * weights
            for k in range(planes):
                own = jnp.where(ours == k, power, 0.0)
                light[k, g * GROUP:(g + 1) * GROUP] += jnp.sum(own, axis=1)
            if step == srcs - 1 and (g + 1) * GROUP % half == 0:
                ship(g * GROUP // half)
    for s in range(srcs):
        rim_out[s] = rims[s]
    for at, peer in enumerate(peers):
        copy = pltpu.make_async_remote_copy(
            rim_out.at[peer], rim_in.at[src], rim_send.at[at], rim_recv.at[at],
            device_id=(tile, peer), device_id_type=MESH)
        copy.start()
        copies.append(copy)
    rim_in[src] = rim_out[src]
    for copy in load_copies:
        copy.wait()
    for copy in filt_copies:
        copy.wait_send()

    row = lax.broadcasted_iota(jnp.int32, (tall, wide), 0) + (tile * rows - halo)
    col = lax.broadcasted_iota(jnp.int32, (tall, wide), 1)
    col = src * block + jnp.where(col < block + 64, col, col - wide)
    inside = (row >= 0) & (row < tiles * rows) & (col >= 0) & (col < cols)
    inside = jnp.where(inside, 1.0, 0.0)
    for copy in copies:
        copy.wait()

    depth = srcs * planes
    for k in range(depth):
        sent = rim_in[k // planes]
        rim = []
        for g in range(tall // GROUP):
            shift = 2 * halo * (k % planes * (tall // GROUP) + g)
            rim.append(pltpu.roll(sent, 128 - shift, 1) if shift else sent)
        main = jnp.concatenate([light_in[h, k // planes, k % planes] for h in range(2)], axis=0)
        exposed = jnp.concatenate(
            [main.astype(jnp.float32), jnp.concatenate(rim, axis=0)], axis=1)
        acid[0, k] = (1.0 - jnp.exp(-exposed)) * inside
        quench[0, k] = loads[k // planes, k % planes:k % planes + 1, 0:1] * inside
        dose[k] = jnp.zeros((rows, block), jnp.float32)

    def blend(centre, sides, vertical, lateral_rate, vertical_rate):
        stay = 1.0 - 4.0 * lateral_rate - 2.0 * vertical_rate
        return stay * centre + lateral_rate * sides + vertical_rate * vertical

    def spread(held, now, k, lateral_rate, vertical_rate):
        centre = held[now, k]
        sides = (
            pltpu.roll(centre, 1, 0) + pltpu.roll(centre, tall - 1, 0)
            + pltpu.roll(centre, 1, 1) + pltpu.roll(centre, wide - 1, 1)
        )
        vertical = held[now, min(k + 1, depth - 1)] + held[now, max(k - 1, 0)]
        return centre, blend(centre, sides, vertical, lateral_rate, vertical_rate)

    def one_step(now):
        for k in range(depth):
            a, a_next = spread(acid, now, k, acid_lateral, acid_vertical)
            q, q_next = spread(quench, now, k, quench_lateral, quench_vertical)
            reacted = react_rate * a * q
            a_next = (a_next - reacted) * inside
            acid[1 - now, k] = a_next
            quench[1 - now, k] = (q_next - reacted) * inside
            dose[k] = dose[k] + a_next[halo:halo + rows, :block]

    def two_steps(pair, carry):
        one_step(0)
        one_step(1)
        return carry

    lax.fori_loop(0, STEPS // 2 - 1, two_steps, 0)
    one_step(0)

    def final_copy(s, slot):
        return pltpu.make_async_remote_copy(
            final_out.at[s], final_in.at[slot], final_send.at[s], final_recv.at[slot],
            device_id=(tile, s), device_id_type=MESH)

    own = slice(halo, halo + rows)
    for s in range(srcs):
        for k in range(s * planes, (s + 1) * planes):
            strip = acid[1, k, own]
            centre = strip[:, :block]
            sides = (
                acid[1, k, halo - 1:halo + rows - 1, :block] + acid[1, k, halo + 1:halo + rows + 1, :block]
                + pltpu.roll(strip, 1, 1)[:, :block] + pltpu.roll(strip, wide - 1, 1)[:, :block]
            )
            vertical = acid[1, min(k + 1, depth - 1), own, :block] + acid[1, max(k - 1, 0), own, :block]
            reacted = react_rate * centre * quench[1, k, own, :block]
            a_next = blend(centre, sides, vertical, acid_lateral, acid_vertical) - reacted
            final_out[s, 0, k % planes] = a_next
            final_out[s, 1, k % planes] = dose[k] + a_next

        @pl.when(src != s)
        def _():
            final_copy(s, src).start()

        @pl.when(src == s)
        def _():
            final_in[s] = final_out[s]

    def place_copy(s):
        return pltpu.make_async_copy(
            final_in.at[s], out_hbm.at[:, :, :, s * block:(s + 1) * block], out_sem.at[s])

    for s in range(srcs):
        @pl.when(src != s)
        def _():
            final_copy(s, s).wait_recv()

        place_copy(s).start()
    for s in range(srcs):
        place_copy(s).wait()

        @pl.when(src != s)
        def _():
            final_copy(s, src).wait_send()


def shards(mask_tiles, kernels, source_weight, dill_rate, quencher_load):
    tiles, srcs = lax.axis_size("tile"), lax.axis_size("src")
    rows, cols = mask_tiles.shape
    planes = dill_rate.shape[0]
    points, parts, depth, quad, side, _ = kernels.shape
    share = planes * points * parts
    raw = kernels.transpose(0, 1, 2, 4, 3, 5).reshape(-1, side)
    dims = (tiles, srcs, rows, cols, side, planes, 1.0 / (24.0 * points * srcs))
    tall = rows + 2 * STEPS
    block = cols // srcs
    wide = block + 128
    depth_all = srcs * planes
    f32 = jnp.float32
    image_rows = 3 * rows
    deep_rows = max(image_rows * SLAB, (tall - GROUP) * SLAB + DEEP)
    out = jax.ShapeDtypeStruct((2, planes, rows, cols), f32)
    dma = pltpu.SemaphoreType.DMA
    result = pl.pallas_call(
        functools.partial(kernel, dims),
        out_shape=out,
        in_specs=[pl.BlockSpec(memory_space=pltpu.HBM)] * 5,
        out_specs=pl.BlockSpec(memory_space=pl.ANY),
        scratch_shapes=[
            pltpu.VMEM(mask_tiles.shape, jnp.int32),
            pltpu.VMEM(raw.shape, jnp.bfloat16),
            pltpu.SMEM(source_weight.shape, jnp.int32),
            pltpu.SMEM(dill_rate.shape, f32),
            pltpu.SMEM(quencher_load.shape, f32),
            pltpu.VMEM((rows, cols), jnp.int32),
            pltpu.VMEM((rows, cols), jnp.int32),
            pltpu.VMEM((raw.shape[0], 128), f32),
            pltpu.VMEM((2, WIRE // 128, srcs * share, 128), f32),
            pltpu.VMEM((2, WIRE // 128, srcs * share, 128), f32),
            pltpu.VMEM((srcs, 2 * share, WIRE), jnp.bfloat16),
            pltpu.VMEM((8, 128), f32),
            pltpu.VMEM((srcs, 2 * share, WIRE), jnp.bfloat16),
            pltpu.VMEM((srcs, 8, 128), f32),
            pltpu.VMEM((cols // 128, deep_rows, 128), f32),
            pltpu.VMEM((tall // GROUP, DEEP, cols), jnp.bfloat16),
            pltpu.VMEM((GROUP * 2 * share, DEEP), jnp.bfloat16),
            pltpu.VMEM((planes, tall, cols), f32),
            pltpu.VMEM((2, srcs, planes, tall // 2, block), jnp.bfloat16),
            pltpu.VMEM((2, srcs, planes, tall // 2, block), jnp.bfloat16),
            pltpu.VMEM((srcs, GROUP, 128), f32),
            pltpu.VMEM((srcs, GROUP, 128), f32),
            pltpu.VMEM((2, depth_all, tall, wide), f32),
            pltpu.VMEM((2, depth_all, tall, wide), f32),
            pltpu.VMEM((depth_all, rows, block), f32),
            pltpu.VMEM((srcs, 2, planes, rows, block), f32),
            pltpu.VMEM((srcs, 2, planes, rows, block), f32),
            dma((5,)), dma((srcs,)), dma((2,)), dma((2,)),
            dma((srcs - 1,)), dma((srcs - 1,)),
            dma((srcs - 1,)), dma((srcs - 1,)),
            dma((2, srcs - 1)), dma((2, srcs - 1)),
            dma((srcs - 1,)), dma((srcs - 1,)),
            dma((srcs,)), dma((srcs,)),
        ],
        compiler_params=pltpu.CompilerParams(
            collective_id=0, has_side_effects=True, vmem_limit_bytes=60 * 1024 * 1024
        ),
    )(mask_tiles, raw, source_weight, dill_rate, quencher_load)
    return result[0], jnp.exp(-deprotect_rate * result[1])


def solution(mesh):
    in_specs = (
        P("tile", None),
        P("src", None, None, None, None, None),
        P("src"),
        P("src"),
        P("src"),
    )
    out_specs = (P("src", "tile", None), P("src", "tile", None))
    return jax.shard_map(shards, mesh=mesh, in_specs=in_specs, out_specs=out_specs, check_vma=False)
```

```python
import functools

import jax
import jax.numpy as jnp
from jax import lax
from jax.experimental import pallas as pl
from jax.experimental.pallas import tpu as pltpu
from jax.sharding import PartitionSpec as P

STEPS = 8
SLAB = 21
DEEP = 512
WIRE = 384
GROUP = 8

acid_lateral = 0.15
acid_vertical = 0.12
quench_lateral = 0.05
quench_vertical = 0.04
react_rate = 0.3
deprotect_rate = 0.25

MESH = pl.DeviceIdType.MESH


def kernel(
    dims,
    mask_hbm, raw_hbm, pupil_hbm, dill_hbm, quench_hbm, out_hbm,
    mask_ref, raw_ref, pupil_ref, dill_ref, quench_ref, above, below, raw, unsorted, sorted_rows, filt_out, load_out, filters, loads, shifted, patches, taps,
    light, light_out, light_in, rim_out, rim_in,
    acid, quench, dose, final_out, final_in,
    here_sem, out_sem, mask_send, mask_recv, filt_send, filt_recv, load_send, load_recv,
    light_send, light_recv, rim_send, rim_recv, final_send, final_recv,
):
    tiles, srcs, rows, cols, side, planes, scale = dims
    rim = side // 2
    halo = STEPS
    tall = rows + 2 * halo
    block = cols // srcs
    wide = block + 128
    local = [
        pltpu.make_async_copy(there, here, here_sem.at[at])
        for at, (there, here) in enumerate((
            (raw_hbm, raw_ref), (pupil_hbm, pupil_ref), (quench_hbm, quench_ref),
            (mask_hbm, mask_ref), (dill_hbm, dill_ref)))
    ]
    for copy in local:
        copy.start()
    tile = lax.axis_index("tile")
    src = lax.axis_index("src")
    has_above = tile > 0
    has_below = tile < tiles - 1

    barrier = pltpu.get_barrier_semaphore()
    peers = [lax.rem(src + step, srcs) for step in range(1, srcs)]
    for peer in peers:
        pl.semaphore_signal(barrier, inc=1, device_id=(tile, peer), device_id_type=MESH)

    @pl.when(has_above)
    def _():
        pl.semaphore_signal(barrier, inc=1, device_id=(tile - 1, src), device_id_type=MESH)

    @pl.when(has_below)
    def _():
        pl.semaphore_signal(barrier, inc=1, device_id=(tile + 1, src), device_id_type=MESH)

    raw[...] = jnp.zeros_like(raw)
    shifted[...] = jnp.zeros_like(shifted)
    for copy in local:
        copy.wait()
    lanes = 128
    points, parts = pupil_ref.shape[0], raw_ref.shape[0] // (2 * side * srcs * planes * pupil_ref.shape[0])
    channels = srcs * planes * points * parts
    share = planes * points * parts
    lane = lax.broadcasted_iota(jnp.int32, (channels, lanes), 1)
    point = lax.broadcasted_iota(jnp.int32, (channels, lanes), 0) // (srcs * planes * parts)
    weight = jnp.zeros((channels, lanes), jnp.float32)
    for p in range(points):
        weight = jnp.where(point == p, pupil_ref[p].astype(jnp.float32), weight)
    weight = jnp.where(lane == lanes - 1, weight, 0.0)
    def widen(at, carry):
        here = pl.ds(pl.multiple_of(at * channels, channels), channels)
        raw[here, :side] = raw_ref[here, :].astype(jnp.float32)
        return carry

    lax.fori_loop(0, 2 * side, widen, 0, unroll=True)
    for q in range(2):
        strips = [jnp.zeros((channels, lanes), jnp.float32) for _ in range(WIRE // lanes)]
        strips[-1] = weight
        for a in range(side):
            part = raw[pl.ds(2 * a + q, channels, 2 * side), :]
            at, offset = divmod(a * SLAB, lanes)
            if offset:
                part = pltpu.roll(part, offset, 1)
            if offset + side > lanes:
                strips[at + 1] = strips[at + 1] + jnp.where(lane < offset, part, 0.0)
                part = jnp.where(lane >= offset, part, 0.0)
            strips[at] = strips[at] + part
        for c, strip in enumerate(strips):
            unsorted[q, c] = strip
            for k in range(srcs * planes):
                sorted_rows[q, c, k * points * parts:(k + 1) * points * parts] = unsorted[
                    q, c, pl.ds(k, points * parts, srcs * planes), :]
            for s in range(srcs):
                filt_out[s, q * share:(q + 1) * share, c * lanes:(c + 1) * lanes] = sorted_rows[
                    q, c, s * share:(s + 1) * share].astype(jnp.bfloat16)
    plane = lax.broadcasted_iota(jnp.int32, load_out.shape, 0)
    spread_load = jnp.zeros(load_out.shape, jnp.float32)
    for k in range(planes):
        spread_load = jnp.where(plane == k, quench_ref[k], spread_load)
    load_out[...] = spread_load

    greeted = srcs - 1 + jnp.where(has_above, 1, 0) + jnp.where(has_below, 1, 0)
    pl.semaphore_wait(barrier, greeted)

    def to_above():
        return pltpu.make_async_remote_copy(
            mask_ref, below, mask_send.at[0], mask_recv.at[0],
            device_id=(tile - 1, src), device_id_type=MESH)

    def to_below():
        return pltpu.make_async_remote_copy(
            mask_ref, above, mask_send.at[1], mask_recv.at[1],
            device_id=(tile + 1, src), device_id_type=MESH)

    @pl.when(has_above)
    def _():
        to_above().start()

    @pl.when(has_below)
    def _():
        to_below().start()

    filt_copies = []
    load_copies = []
    for at, peer in enumerate(peers):
        copy = pltpu.make_async_remote_copy(
            filt_out.at[peer], filters.at[src], filt_send.at[at], filt_recv.at[at],
            device_id=(tile, peer), device_id_type=MESH)
        copy.start()
        filt_copies.append(copy)
        copy = pltpu.make_async_remote_copy(
            load_out, loads.at[src], load_send.at[at], load_recv.at[at],
            device_id=(tile, peer), device_id_type=MESH)
        copy.start()
        load_copies.append(copy)
    filters[src] = filt_out[src]
    loads[src] = load_out[...]

    @pl.when(jnp.logical_not(has_above))
    def _():
        above[...] = jnp.zeros_like(above)

    @pl.when(jnp.logical_not(has_below))
    def _():
        below[...] = jnp.zeros_like(below)

    @pl.when(has_above)
    def _():
        to_above().wait_send()
        to_below().wait_recv()

    @pl.when(has_below)
    def _():
        to_below().wait_send()
        to_above().wait_recv()

    image = jnp.concatenate([above[...], mask_ref[...], below[...]], axis=0).astype(jnp.float32)
    ring = jnp.concatenate([image, jnp.zeros((image.shape[0], 128), jnp.float32)], axis=1)
    length = cols + 128
    for b in range(side):
        moved = pltpu.roll(ring, (rim - b) % length, 1)[:, :cols]
        for c in range(cols // 128):
            shifted[c, pl.ds(b, image.shape[0], SLAB), :] = moved[:, c * 128:(c + 1) * 128]

    for g in range(tall // GROUP):
        for c in range(cols // 128):
            patches[g, :, c * 128:(c + 1) * 128] = shifted[
                c, g * GROUP * SLAB:g * GROUP * SLAB + DEEP, :].astype(jnp.bfloat16)
    light[...] = jnp.zeros_like(light)

    half = tall // 2
    edge = lax.broadcasted_iota(jnp.int32, (GROUP, 128), 1)
    none = jnp.zeros((GROUP, 128), jnp.float32)
    rims = [none] * srcs
    copies = []

    def ship(h):
        for k in range(planes):
            exposed = light[k, h * half:(h + 1) * half] * (dill_ref[k] * scale)
            for s in range(srcs):
                light_out[h, s, k] = exposed[:, s * block:(s + 1) * block].astype(jnp.bfloat16)
                for g in range(half // GROUP):
                    rows8 = exposed[g * GROUP:(g + 1) * GROUP]
                    right = rows8[:, (s + 1) * block:(s + 1) * block + 128] if s < srcs - 1 else none
                    left = rows8[:, s * block - 128:s * block] if s else none
                    picked = jnp.where(edge < halo, right, jnp.where(edge >= 128 - halo, left, 0.0))
                    shift = 2 * halo * (k * (tall // GROUP) + h * (half // GROUP) + g)
                    rims[s] = rims[s] + (pltpu.roll(picked, shift, 1) if shift else picked)
        for at, peer in enumerate(peers):
            copy = pltpu.make_async_remote_copy(
                light_out.at[h, peer], light_in.at[h, src], light_send.at[h, at], light_recv.at[h, at],
                device_id=(tile, peer), device_id_type=MESH)
            copy.start()
            copies.append(copy)
        light_in[h, src] = light_out[h, src]

    place = lax.broadcasted_iota(jnp.int32, (2 * share, WIRE), 1)
    ours = lax.broadcasted_iota(jnp.int32, (share, cols), 0) // (points * parts)
    for step in range(srcs):
        if step:
            filt_copies[step - 1].wait_recv()
        held = filters[lax.rem(src + srcs - step, srcs)].astype(jnp.float32)
        weights = jnp.sum(jnp.where(place == WIRE - 1, held, 0.0), axis=1, keepdims=True)[:share]
        held = jnp.where(place < side * SLAB, held, 0.0)
        held = jnp.concatenate([held, jnp.zeros((2 * share, DEEP - WIRE), jnp.float32)], axis=1)
        for r in range(GROUP):
            moved = pltpu.roll(held, r * SLAB, 1) if r else held
            taps[r * 2 * share:(r + 1) * 2 * share] = moved.astype(jnp.bfloat16)

        for g in range(tall // GROUP):
            field = jnp.dot(taps[...], patches[g], preferred_element_type=jnp.float32)
            square = (field * field).reshape(GROUP, 2, share, cols)
            power = (square[:, 0] + square[:, 1]) * weights
            for k in range(planes):
                own = jnp.where(ours == k, power, 0.0)
                light[k, g * GROUP:(g + 1) * GROUP] += jnp.sum(own, axis=1)
            if step == srcs - 1 and (g + 1) * GROUP % half == 0:
                ship(g * GROUP // half)
    for s in range(srcs):
        rim_out[s] = rims[s]
    for at, peer in enumerate(peers):
        copy = pltpu.make_async_remote_copy(
            rim_out.at[peer], rim_in.at[src], rim_send.at[at], rim_recv.at[at],
            device_id=(tile, peer), device_id_type=MESH)
        copy.start()
        copies.append(copy)
    rim_in[src] = rim_out[src]
    for copy in load_copies:
        copy.wait()
    for copy in filt_copies:
        copy.wait_send()

    row = lax.broadcasted_iota(jnp.int32, (tall, wide), 0) + (tile * rows - halo)
    col = lax.broadcasted_iota(jnp.int32, (tall, wide), 1)
    col = src * block + jnp.where(col < block + 64, col, col - wide)
    inside = (row >= 0) & (row < tiles * rows) & (col >= 0) & (col < cols)
    inside = jnp.where(inside, 1.0, 0.0)
    for copy in copies:
        copy.wait()

    depth = srcs * planes
    for k in range(depth):
        sent = rim_in[k // planes]
        rim = []
        for g in range(tall // GROUP):
            shift = 2 * halo * (k % planes * (tall // GROUP) + g)
            rim.append(pltpu.roll(sent, 128 - shift, 1) if shift else sent)
        main = jnp.concatenate([light_in[h, k // planes, k % planes] for h in range(2)], axis=0)
        exposed = jnp.concatenate(
            [main.astype(jnp.float32), jnp.concatenate(rim, axis=0)], axis=1)
        acid[0, k] = (1.0 - jnp.exp(-exposed)) * inside
        quench[0, k] = loads[k // planes, k % planes:k % planes + 1, 0:1] * inside
        dose[k] = jnp.zeros((rows, block), jnp.float32)

    def blend(centre, sides, vertical, lateral_rate, vertical_rate):
        stay = 1.0 - 4.0 * lateral_rate - 2.0 * vertical_rate
        return stay * centre + lateral_rate * sides + vertical_rate * vertical

    def spread(held, now, k, lateral_rate, vertical_rate):
        centre = held[now, k]
        sides = (
            pltpu.roll(centre, 1, 0) + pltpu.roll(centre, tall - 1, 0)
            + pltpu.roll(centre, 1, 1) + pltpu.roll(centre, wide - 1, 1)
        )
        vertical = held[now, min(k + 1, depth - 1)] + held[now, max(k - 1, 0)]
        return centre, blend(centre, sides, vertical, lateral_rate, vertical_rate)

    def one_step(now):
        for k in range(depth):
            a, a_next = spread(acid, now, k, acid_lateral, acid_vertical)
            q, q_next = spread(quench, now, k, quench_lateral, quench_vertical)
            reacted = react_rate * a * q
            a_next = (a_next - reacted) * inside
            acid[1 - now, k] = a_next
            quench[1 - now, k] = (q_next - reacted) * inside
            dose[k] = dose[k] + a_next[halo:halo + rows, :block]

    def two_steps(pair, carry):
        one_step(0)
        one_step(1)
        return carry

    lax.fori_loop(0, STEPS // 2 - 1, two_steps, 0)
    one_step(0)

    def final_copy(s, slot):
        return pltpu.make_async_remote_copy(
            final_out.at[s], final_in.at[slot], final_send.at[s], final_recv.at[slot],
            device_id=(tile, s), device_id_type=MESH)

    own = slice(halo, halo + rows)
    for s in range(srcs):
        for k in range(s * planes, (s + 1) * planes):
            strip = acid[1, k, own]
            centre = strip[:, :block]
            sides = (
                acid[1, k, halo - 1:halo + rows - 1, :block] + acid[1, k, halo + 1:halo + rows + 1, :block]
                + pltpu.roll(strip, 1, 1)[:, :block] + pltpu.roll(strip, wide - 1, 1)[:, :block]
            )
            vertical = acid[1, min(k + 1, depth - 1), own, :block] + acid[1, max(k - 1, 0), own, :block]
            reacted = react_rate * centre * quench[1, k, own, :block]
            a_next = blend(centre, sides, vertical, acid_lateral, acid_vertical) - reacted
            final_out[s, 0, k % planes] = a_next
            final_out[s, 1, k % planes] = dose[k] + a_next

        @pl.when(src != s)
        def _():
            final_copy(s, src).start()

        @pl.when(src == s)
        def _():
            final_in[s] = final_out[s]

    def place_copy(s):
        return pltpu.make_async_copy(
            final_in.at[s], out_hbm.at[:, :, :, s * block:(s + 1) * block], out_sem.at[s])

    for s in range(srcs):
        @pl.when(src != s)
        def _():
            final_copy(s, s).wait_recv()

        place_copy(s).start()
    for s in range(srcs):
        place_copy(s).wait()

        @pl.when(src != s)
        def _():
            final_copy(s, src).wait_send()


def shards(mask_tiles, kernels, source_weight, dill_rate, quencher_load):
    tiles, srcs = lax.axis_size("tile"), lax.axis_size("src")
    rows, cols = mask_tiles.shape
    planes = dill_rate.shape[0]
    points, parts, depth, quad, side, _ = kernels.shape
    share = planes * points * parts
    raw = kernels.transpose(0, 1, 2, 4, 3, 5).reshape(-1, side)
    dims = (tiles, srcs, rows, cols, side, planes, 1.0 / (24.0 * points * srcs))
    tall = rows + 2 * STEPS
    block = cols // srcs
    wide = block + 128
    depth_all = srcs * planes
    f32 = jnp.float32
    image_rows = 3 * rows
    deep_rows = max(image_rows * SLAB, (tall - GROUP) * SLAB + DEEP)
    out = jax.ShapeDtypeStruct((2, planes, rows, cols), f32)
    dma = pltpu.SemaphoreType.DMA
    result = pl.pallas_call(
        functools.partial(kernel, dims),
        out_shape=out,
        in_specs=[pl.BlockSpec(memory_space=pltpu.HBM)] * 5,
        out_specs=pl.BlockSpec(memory_space=pl.ANY),
        scratch_shapes=[
            pltpu.VMEM(mask_tiles.shape, jnp.int32),
            pltpu.VMEM(raw.shape, jnp.bfloat16),
            pltpu.SMEM(source_weight.shape, jnp.int32),
            pltpu.SMEM(dill_rate.shape, f32),
            pltpu.SMEM(quencher_load.shape, f32),
            pltpu.VMEM((rows, cols), jnp.int32),
            pltpu.VMEM((rows, cols), jnp.int32),
            pltpu.VMEM((raw.shape[0], 128), f32),
            pltpu.VMEM((2, WIRE // 128, srcs * share, 128), f32),
            pltpu.VMEM((2, WIRE // 128, srcs * share, 128), f32),
            pltpu.VMEM((srcs, 2 * share, WIRE), jnp.bfloat16),
            pltpu.VMEM((8, 128), f32),
            pltpu.VMEM((srcs, 2 * share, WIRE), jnp.bfloat16),
            pltpu.VMEM((srcs, 8, 128), f32),
            pltpu.VMEM((cols // 128, deep_rows, 128), f32),
            pltpu.VMEM((tall // GROUP, DEEP, cols), jnp.bfloat16),
            pltpu.VMEM((GROUP * 2 * share, DEEP), jnp.bfloat16),
            pltpu.VMEM((planes, tall, cols), f32),
            pltpu.VMEM((2, srcs, planes, tall // 2, block), jnp.bfloat16),
            pltpu.VMEM((2, srcs, planes, tall // 2, block), jnp.bfloat16),
            pltpu.VMEM((srcs, GROUP, 128), f32),
            pltpu.VMEM((srcs, GROUP, 128), f32),
            pltpu.VMEM((2, depth_all, tall, wide), f32),
            pltpu.VMEM((2, depth_all, tall, wide), f32),
            pltpu.VMEM((depth_all, rows, block), f32),
            pltpu.VMEM((srcs, 2, planes, rows, block), f32),
            pltpu.VMEM((srcs, 2, planes, rows, block), f32),
            dma((5,)), dma((srcs,)), dma((2,)), dma((2,)),
            dma((srcs - 1,)), dma((srcs - 1,)),
            dma((srcs - 1,)), dma((srcs - 1,)),
            dma((2, srcs - 1)), dma((2, srcs - 1)),
            dma((srcs - 1,)), dma((srcs - 1,)),
            dma((srcs,)), dma((srcs,)),
        ],
        compiler_params=pltpu.CompilerParams(
            collective_id=0, has_side_effects=True, vmem_limit_bytes=60 * 1024 * 1024
        ),
    )(mask_tiles, raw, source_weight, dill_rate, quencher_load)
    return result[0], jnp.exp(-deprotect_rate * result[1])


def solution(mesh):
    in_specs = (
        P("tile", None),
        P("src", None, None, None, None, None),
        P("src"),
        P("src"),
        P("src"),
    )
    out_specs = (P("src", "tile", None), P("src", "tile", None))
    return jax.shard_map(shards, mesh=mesh, in_specs=in_specs, out_specs=out_specs, check_vma=False)
```
